32 devices in a mesh: seq: 4 (over z), head: 8 (over y, x, core).
Axes of the slice: x: 2, y: 2, z: 4, core: 2. Of those that a mesh axis runs over, the one named last changes fastest.
Arguments:
- queries: bfloat16 [4096, 1024], P(('seq', 'head')), may hold values from -6 to 6
- keys: bfloat16 [4096, 256], P(('seq', 'head')), may hold values from -6 to 6
- values: bfloat16 [4096, 256], P(('seq', 'head')), may hold values from -6 to 6
- out_grad: bfloat16 [4096, 1024], P(('seq', 'head')), may hold values from -6 to 6
Outputs:
- queries_grad: bfloat16 [4096, 1024], P(('seq', 'head'))
- keys_grad: bfloat16 [4096, 256], P(('seq', 'head'))
- values_grad: bfloat16 [4096, 256], P(('seq', 'head'))
The draws below stay inside these ranges and needn't reach their ends.
All inputs are finite; a program needn't handle non-finite values.
Results may differ from the reference program's by a relative error of at most 0.0065.
Values may be sent and summed in bfloat16 or wider, within the bound.
No kernel may reach another device: no remote copies, remote signals or barrier semaphores. Data moves between devices by JAX's collectives and lax.ppermute only.
A program may use at most 64 MiB of HBM per device.

```python
import jax
import jax.numpy as jnp
from jax import lax

HD = 128
GROUP = 4
BLK = 256
HEADS = 8
KV_HEADS = 2
TOKENS = 4096


def levels(stream_key, dims, cuts, least, top_value):
    level, own = 1.0, jax.random.fold_in(stream_key, 6)
    for axis_at, parts in cuts:
        draws = jnp.exp(jax.random.uniform(jax.random.fold_in(own, axis_at), (parts,), jnp.float32, least / len(cuts), top_value / len(cuts)))
        level = level * jnp.repeat(draws, dims[axis_at] // parts).reshape([-1 if axis == axis_at else 1 for axis in range(len(dims))])
    return level


def bell_draw(stream_key, extent, width, reach, shards=(), kind=jnp.bfloat16):
    gain = levels(stream_key, extent, shards, -0.22, 0.18) if shards else 1.0
    entries = jax.random.normal(stream_key, extent, jnp.float32) * width * gain
    return jnp.minimum(jnp.maximum(entries, -reach), reach).astype(kind)


def setup_inputs(seed: int = 0) -> dict:
    key_of = jax.random.split(jax.random.key(seed), 5)
    return {
        "queries": bell_draw(key_of[0], (TOKENS, HEADS * HD), 1.0, 6.0, ((0, 32),)),
        "keys": bell_draw(key_of[1], (TOKENS, KV_HEADS * HD), 1.0, 6.0, ((0, 32),)),
        "values": bell_draw(key_of[2], (TOKENS, KV_HEADS * HD), 1.0, 6.0, ((0, 32),)),
        "out_grad": bell_draw(key_of[3], (TOKENS, HEADS * HD), 1.0, 6.0, ((0, 32),)),
    }


def exclusive_forward(states):
    running = jnp.cumsum(states, axis=0)
    return jnp.concatenate([jnp.zeros_like(states[:1]), running[:-1]], axis=0)

def exclusive_backward(states):
    running = jnp.cumsum(states[::-1], axis=0)[::-1]
    return jnp.concatenate([running[1:], jnp.zeros_like(states[:1])], axis=0)

def reference(queries, keys, values, out_grad):
    positions = jnp.arange(TOKENS, dtype=jnp.int32)
    scale = 1.0 / jnp.sqrt((HD * (positions + 1)).astype(jnp.float32))
    block_count = TOKENS // BLK
    causal = jnp.arange(BLK)[:, None] >= jnp.arange(BLK)[None, :]
    scale_blocks = scale.reshape(block_count, BLK)

    def one_block(pieces):
        query_block, key_block, value_block, cot_block, scaled_block, scale_block, prior_state, future_state = pieces
        key_scores = jnp.dot(query_block, key_block.T, preferred_element_type=jnp.float32)
        forward_weights = jnp.where(causal, scale_block[:, None] * key_scores, 0.0).astype(jnp.bfloat16)
        value_scores = jnp.dot(scaled_block, value_block.T, preferred_element_type=jnp.float32)
        backward_weights = jnp.where(causal, value_scores, 0.0).astype(jnp.bfloat16)
        query_grad = jnp.dot(backward_weights, key_block, preferred_element_type=jnp.float32)
        query_grad = query_grad + jnp.dot(scaled_block, prior_state.T, preferred_element_type=jnp.float32)
        key_grad = jnp.dot(backward_weights.T, query_block, preferred_element_type=jnp.float32)
        key_grad = key_grad + jnp.dot(value_block, future_state, preferred_element_type=jnp.float32)
        value_grad = jnp.dot(forward_weights.T, cot_block, preferred_element_type=jnp.float32)
        value_grad = value_grad + jnp.dot(key_block, future_state.T, preferred_element_type=jnp.float32)
        return (query_grad.astype(jnp.bfloat16), key_grad.astype(jnp.bfloat16), value_grad.astype(jnp.bfloat16))

    def head_grads(head):
        kv_index = head // GROUP
        query_cols = lax.dynamic_slice_in_dim(queries, (head * HD).astype(jnp.int32), HD, 1)
        cot_cols = lax.dynamic_slice_in_dim(out_grad, (head * HD).astype(jnp.int32), HD, 1)
        key_cols = lax.dynamic_slice_in_dim(keys, (kv_index * HD).astype(jnp.int32), HD, 1)
        value_cols = lax.dynamic_slice_in_dim(values, (kv_index * HD).astype(jnp.int32), HD, 1)
        scaled_cot = (scale[:, None] * cot_cols.astype(jnp.float32)).astype(jnp.bfloat16)
        query_blocks = query_cols.reshape(block_count, BLK, HD)
        key_blocks = key_cols.reshape(block_count, BLK, HD)
        value_blocks = value_cols.reshape(block_count, BLK, HD)
        cot_blocks = cot_cols.reshape(block_count, BLK, HD)
        scaled_blocks = scaled_cot.reshape(block_count, BLK, HD)
        pair_states = jnp.einsum('bsd,bse->bde', key_blocks.astype(jnp.float32), value_blocks.astype(jnp.float32), precision=lax.Precision.HIGHEST)
        grad_states = jnp.einsum('bte,btd->bed', scaled_blocks.astype(jnp.float32), query_blocks.astype(jnp.float32), precision=lax.Precision.HIGHEST)
        prior_states = exclusive_forward(pair_states).astype(jnp.bfloat16)
        future_states = exclusive_backward(grad_states).astype(jnp.bfloat16)
        return lax.map(one_block, (query_blocks, key_blocks, value_blocks, cot_blocks, scaled_blocks, scale_blocks, prior_states, future_states))
    query_grad, key_grad, value_grad = lax.map(head_grads, jnp.arange(HEADS, dtype=jnp.int32))
    queries_grad = query_grad.reshape(HEADS, TOKENS, HD).transpose(1, 0, 2).reshape(TOKENS, HEADS * HD)
    key_sum = lax.optimization_barrier(jnp.sum(key_grad.reshape(KV_HEADS, GROUP, TOKENS, HD).astype(jnp.float32), axis=1)).astype(jnp.bfloat16)
    value_sum = lax.optimization_barrier(jnp.sum(value_grad.reshape(KV_HEADS, GROUP, TOKENS, HD).astype(jnp.float32), axis=1)).astype(jnp.bfloat16)
    keys_grad = key_sum.transpose(1, 0, 2).reshape(TOKENS, KV_HEADS * HD)
    values_grad = value_sum.transpose(1, 0, 2).reshape(TOKENS, KV_HEADS * HD)
    return (queries_grad, keys_grad, values_grad)
```

```python
import functools

import jax
import jax.numpy as jnp
from jax import lax
from jax.experimental import pallas as pl
from jax.experimental.pallas import tpu as pltpu
from jax.sharding import PartitionSpec as P

HD = 128
SEQ = "seq"
HEAD = "head"
BF16 = jnp.bfloat16
F32 = jnp.float32

NN = (((1,), (0,)), ((), ()))
NT = (((1,), (1,)), ((), ()))
TN = (((0,), (0,)), ((), ()))


def dot(left, right, dims):
    return lax.dot_general(left, right, dims, preferred_element_type=F32)


def columns(ref, index):
    return ref[:, index * HD : (index + 1) * HD]


def row_scale(start, tokens, shape, axis):
    positions = start + lax.broadcasted_iota(jnp.int32, shape, axis)
    return 1.0 / jnp.sqrt((HD * (positions + 1)).astype(F32))


def first_token(tokens):
    device = lax.axis_index(SEQ) * lax.axis_size(HEAD) + lax.axis_index(HEAD)
    return device * tokens


def states_kernel(q_ref, k_ref, v_ref, o_ref, keep_ref, send_ref):
    tokens = q_ref.shape[0]
    kv = k_ref.shape[1] // HD
    group = q_ref.shape[1] // HD // kv
    half = kv // 2
    core = lax.rem(lax.axis_index(HEAD), 2)
    scale = row_scale(first_token(tokens), tokens, (tokens, HD), 0)
    made = []
    for g in range(kv):
        pair = dot(columns(v_ref, g), columns(k_ref, g), TN)
        grad = jnp.zeros((HD, HD), F32)
        for h in range(g * group, (g + 1) * group):
            scaled = (scale * columns(o_ref, h).astype(F32)).astype(BF16)
            grad = grad + dot(scaled, columns(q_ref, h), TN)
        made.append((pair.astype(BF16), grad.astype(BF16)))

    def put(ref, first):
        for g in range(half):
            ref[0, g] = made[first + g][0]
            ref[1, g] = made[first + g][1]

    @pl.when(core == 0)
    def _():
        put(keep_ref, 0)
        put(send_ref, half)

    @pl.when(core == 1)
    def _():
        put(keep_ref, half)
        put(send_ref, 0)


def grads_kernel(q_ref, k_ref, v_ref, o_ref, mine_ref, other_ref, qg_ref, kg_ref, vg_ref, carried):
    tokens = q_ref.shape[0]
    kv = k_ref.shape[1] // HD
    group = q_ref.shape[1] // HD // kv
    half = kv // 2
    core = lax.rem(lax.axis_index(HEAD), 2)
    carried[core] = mine_ref[...]
    carried[1 - core] = other_ref[...]
    start = first_token(tokens)
    scale = row_scale(start, tokens, (tokens, HD), 0)
    scale_row = row_scale(start, tokens, (HD, tokens), 1)
    causal = lax.broadcasted_iota(jnp.int32, (tokens, tokens), 0) >= lax.broadcasted_iota(
        jnp.int32, (tokens, tokens), 1
    )
    causal_t = lax.broadcasted_iota(jnp.int32, (tokens, tokens), 0) <= lax.broadcasted_iota(
        jnp.int32, (tokens, tokens), 1
    )
    for g in range(kv):
        key = columns(k_ref, g)
        value = columns(v_ref, g)
        prior = carried[g // half, 0, g % half]
        future = carried[g // half, 1, g % half]
        key_grad = dot(value, future, NN)
        value_grad = dot(key, future, NT)
        for h in range(g * group, (g + 1) * group):
            query = columns(q_ref, h)
            cot = columns(o_ref, h)
            scaled = (scale * cot.astype(F32)).astype(BF16)
            backward = jnp.where(causal, dot(scaled, value, NT), 0.0).astype(BF16)
            backward_t = jnp.where(causal_t, dot(value, scaled, NT), 0.0).astype(BF16)
            forward_t = jnp.where(causal_t, scale_row * dot(key, query, NT), 0.0).astype(BF16)
            query_grad = dot(backward, key, NN) + dot(scaled, prior, NN)
            qg_ref[:, h * HD : (h + 1) * HD] = query_grad.astype(BF16)
            key_grad = key_grad + dot(backward_t, query, NN)
            value_grad = value_grad + dot(forward_t, cot, NN)
        kg_ref[:, g * HD : (g + 1) * HD] = key_grad.astype(BF16)
        vg_ref[:, g * HD : (g + 1) * HD] = value_grad.astype(BF16)


def digits(size):
    bits = size.bit_length() - 1
    assert 1 << bits == size
    shifts = []
    while bits > 0:
        width = 2 if bits >= 2 else 1
        bits -= width
        shifts.append((bits, width))
    return shifts


def carry_states(keep, send):
    head_count = lax.axis_size(HEAD)
    head_index = lax.axis_index(HEAD)
    core = lax.rem(head_index, 2)
    swap = [(i, i ^ 1) for i in range(head_count)]
    got = lax.ppermute(send, HEAD, swap).astype(F32)
    keep = keep.astype(F32)
    chip = keep + got
    steps = [(SEQ, lax.axis_size(SEQ), lax.axis_index(SEQ), digit) for digit in digits(lax.axis_size(SEQ))]
    steps += [
        (HEAD, head_count, head_index, (shift + 1, width)) for shift, width in digits(head_count // 2)
    ]
    carried = None
    for axis, size, index, (shift, width) in steps:
        received = []
        for flip in range(1, 1 << width):
            mask = flip << shift
            lower = index < (index ^ mask)
            perm = [(i, i ^ mask) for i in range(size)]
            if carried is None:
                message = jnp.where(lower, chip[0], chip[1]).astype(BF16)
                arrived = lax.ppermute(message, axis, perm).astype(F32)
                received.append(
                    jnp.stack([jnp.where(lower, 0.0, arrived), jnp.where(lower, arrived, 0.0)])
                )
            else:
                message = jnp.stack(
                    [
                        carried[0] + jnp.where(lower, chip[0], 0.0),
                        carried[1] + jnp.where(lower, 0.0, chip[1]),
                    ]
                ).astype(BF16)
                received.append(lax.ppermute(message, axis, perm).astype(F32))
        total = functools.reduce(jnp.add, received)
        carried = total if carried is None else carried + total
    first = core == 0
    mine = jnp.stack(
        [carried[0] + jnp.where(first, 0.0, got[0]), carried[1] + jnp.where(first, got[1], 0.0)]
    ).astype(BF16)
    to_other = jnp.stack(
        [carried[0] + jnp.where(first, keep[0], 0.0), carried[1] + jnp.where(first, 0.0, keep[1])]
    ).astype(BF16)
    other = lax.ppermute(to_other, HEAD, swap)
    return mine, other


def body(queries, keys, values, out_grad):
    tokens = queries.shape[0]
    kv = keys.shape[1] // HD
    half = kv // 2
    shape = (2, half, HD, HD)
    vmem = pl.BlockSpec(memory_space=pltpu.VMEM)
    inputs = (queries, keys, values, out_grad)
    keep, send = pl.pallas_call(
        states_kernel,
        out_shape=(jax.ShapeDtypeStruct(shape, BF16),) * 2,
        in_specs=[vmem] * 4,
        out_specs=[vmem] * 2,
        compiler_params=pltpu.CompilerParams(vmem_limit_bytes=32 * 1024 * 1024),
    )(*inputs)
    mine, other = carry_states(keep, send)
    return pl.pallas_call(
        grads_kernel,
        out_shape=tuple(jax.ShapeDtypeStruct(x.shape, BF16) for x in (queries, keys, values)),
        in_specs=[vmem] * 6,
        out_specs=[vmem] * 3,
        scratch_shapes=[pltpu.VMEM((2,) + shape, BF16)],
        compiler_params=pltpu.CompilerParams(vmem_limit_bytes=32 * 1024 * 1024),
    )(*inputs, mine, other)


def solution(mesh):
    spec = P((SEQ, HEAD), None)
    return jax.shard_map(
        body, mesh=mesh, in_specs=(spec,) * 4, out_specs=(spec,) * 3, check_vma=False
    )
```

```python
import functools

import jax
import jax.numpy as jnp
from jax import lax
from jax.experimental import pallas as pl
from jax.experimental.pallas import tpu as pltpu
from jax.sharding import PartitionSpec as P

HD = 128
SEQ = "seq"
HEAD = "head"
DEVICES = (SEQ, HEAD)
TOP_BITS = 2
LOW_BITS = 2
MIB = 1024 * 1024
BF16 = jnp.bfloat16
F32 = jnp.float32

NN = (((1,), (0,)), ((), ()))
NT = (((1,), (1,)), ((), ()))
TN = (((0,), (0,)), ((), ()))


def dot(left, right, dims):
    return lax.dot_general(left, right, dims, preferred_element_type=F32)


def columns(index):
    return (slice(None), slice(index * HD, (index + 1) * HD))


def device_index():
    return lax.axis_index(SEQ) * lax.axis_size(HEAD) + lax.axis_index(HEAD)


def row_scale(tokens, shape, axis):
    positions = device_index() * tokens + lax.broadcasted_iota(jnp.int32, shape, axis)
    return 1.0 / jnp.sqrt((HD * (positions + 1)).astype(F32))


def states_kernel(q_hbm, k_hbm, v_hbm, o_hbm, keep_ref, send_ref, q_ref, k_ref, v_ref, o_ref, sems):
    tokens = q_hbm.shape[0]
    kv = k_hbm.shape[1] // HD
    width = q_hbm.shape[1] // kv
    group = width // HD
    half = kv // 2
    small = [
        pltpu.make_async_copy(k_hbm, k_ref, sems.at[0, 0]),
        pltpu.make_async_copy(v_hbm, v_ref, sems.at[1, 0]),
    ]
    large = []
    for g in range(kv):
        at = (slice(None), slice(g * width, (g + 1) * width))
        large.append(
            [
                pltpu.make_async_copy(o_hbm.at[at], o_ref.at[at], sems.at[0, 1 + g]),
                pltpu.make_async_copy(q_hbm.at[at], q_ref.at[at], sems.at[1, 1 + g]),
            ]
        )
    for copy in small:
        copy.start()
    for copies in large:
        for copy in copies:
            copy.start()
    core = lax.rem(lax.axis_index(HEAD), 2)
    scale = row_scale(tokens, (tokens, HD), 0)

    def put(g, kind, state):
        mine = core == g // half

        @pl.when(mine)
        def _():
            keep_ref[kind, g % half] = state

        @pl.when(jnp.logical_not(mine))
        def _():
            send_ref[kind, g % half] = state

    for copy in small:
        copy.wait()
    for g in range(kv):
        put(g, 0, dot(v_ref[columns(g)], k_ref[columns(g)], TN).astype(BF16))
    for g in range(kv):
        for copy in large[g]:
            copy.wait()
        grad = jnp.zeros((HD, HD), F32)
        for h in range(g * group, (g + 1) * group):
            scaled = (scale * o_ref[columns(h)].astype(F32)).astype(BF16)
            grad = grad + dot(scaled, q_ref[columns(h)], TN)
        put(g, 1, grad.astype(BF16))


def local_kernel(q_ref, k_ref, v_ref, o_ref, qg_ref, kg_ref, vg_ref):
    tokens = q_ref.shape[0]
    kv = k_ref.shape[1] // HD
    group = q_ref.shape[1] // HD // kv
    scale = row_scale(tokens, (tokens, HD), 0)
    scale_row = row_scale(tokens, (HD, tokens), 1)
    rows = lax.broadcasted_iota(jnp.int32, (tokens, tokens), 0)
    cols = lax.broadcasted_iota(jnp.int32, (tokens, tokens), 1)
    causal = rows >= cols
    causal_t = rows <= cols
    for g in range(kv):
        key = k_ref[columns(g)]
        value = v_ref[columns(g)]
        key_grad = jnp.zeros((tokens, HD), F32)
        value_grad = jnp.zeros((tokens, HD), F32)
        for h in range(g * group, (g + 1) * group):
            query = q_ref[columns(h)]
            cot = o_ref[columns(h)]
            scaled = (scale * cot.astype(F32)).astype(BF16)
            backward = jnp.where(causal, dot(scaled, value, NT), 0.0).astype(BF16)
            backward_t = jnp.where(causal_t, dot(value, scaled, NT), 0.0).astype(BF16)
            forward_t = jnp.where(causal_t, scale_row * dot(key, query, NT), 0.0).astype(BF16)
            qg_ref[columns(h)] = dot(backward, key, NN)
            key_grad = key_grad + dot(backward_t, query, NN)
            value_grad = value_grad + dot(forward_t, cot, NN)
        kg_ref[columns(g)] = key_grad
        vg_ref[columns(g)] = value_grad


def finish_kernel(
    k_ref, v_ref, o_ref, ql_ref, kl_ref, vl_ref, mine_ref, other_ref,
    qg_hbm, kg_hbm, vg_hbm, carried, qg_ref, kg_ref, vg_ref, sems,
):
    tokens = o_ref.shape[0]
    kv = k_ref.shape[1] // HD
    width = o_ref.shape[1] // kv
    group = width // HD
    half = kv // 2
    core = lax.rem(lax.axis_index(HEAD), 2)
    carried[core] = mine_ref[...]
    carried[1 - core] = other_ref[...]
    scale = row_scale(tokens, (tokens, HD), 0)
    copies = []
    for g in range(kv):
        prior = carried[g // half, 0, g % half]
        for h in range(g * group, (g + 1) * group):
            scaled = (scale * o_ref[columns(h)].astype(F32)).astype(BF16)
            qg_ref[columns(h)] = (ql_ref[columns(h)] + dot(scaled, prior, NN)).astype(BF16)
        at = (slice(None), slice(g * width, (g + 1) * width))
        copies.append(pltpu.make_async_copy(qg_ref.at[at], qg_hbm.at[at], sems.at[g]))
        copies[-1].start()
    for g in range(kv):
        future = carried[g // half, 1, g % half]
        key_grad = kl_ref[columns(g)] + dot(v_ref[columns(g)], future, NN)
        value_grad = vl_ref[columns(g)] + dot(k_ref[columns(g)], future, NT)
        kg_ref[columns(g)] = key_grad.astype(BF16)
        vg_ref[columns(g)] = value_grad.astype(BF16)
    copies.append(pltpu.make_async_copy(kg_ref, kg_hbm, sems.at[kv]))
    copies.append(pltpu.make_async_copy(vg_ref, vg_hbm, sems.at[kv + 1]))
    for copy in copies[-2:]:
        copy.start()
    for copy in copies:
        copy.wait()


def bit_groups(size):
    bits = size.bit_length() - 1
    assert 1 << bits == size
    low = list(range(1, max(1, bits - TOP_BITS)))
    groups = [low[i : i + LOW_BITS] for i in range(0, len(low), LOW_BITS)]
    return groups + [list(range(max(1, bits - TOP_BITS), bits))]


def flips_of(group):
    masks = [0]
    for bit in group:
        masks += [mask | 1 << bit for mask in masks]
    return masks[1:]


def carry_states(keep, send):
    size = lax.axis_size(SEQ) * lax.axis_size(HEAD)
    index = device_index()
    swap = [(i, i ^ 1) for i in range(size)]
    got = lax.ppermute(send, DEVICES, swap).astype(F32)
    keep = keep.astype(F32)
    total = keep + got
    earlier = jnp.zeros_like(total[0])
    later = jnp.zeros_like(total[1])
    groups = bit_groups(size)
    for group in groups[:-1]:
        message = total.astype(BF16)
        for flip in flips_of(group):
            arrived = lax.ppermute(message, DEVICES, [(i, i ^ flip) for i in range(size)]).astype(F32)
            lower = index < (index ^ flip)
            earlier = earlier + jnp.where(lower, 0.0, arrived[0])
            later = later + jnp.where(lower, arrived[1], 0.0)
            total = total + arrived
    message = total.astype(BF16)
    for flip in flips_of(groups[-1]):
        lower = index < (index ^ flip)
        arrived = lax.ppermute(
            jnp.where(lower, message[0], message[1]), DEVICES, [(i, i ^ flip) for i in range(size)]
        ).astype(F32)
        earlier = earlier + jnp.where(lower, 0.0, arrived)
        later = later + jnp.where(lower, arrived, 0.0)
    first = index % 2 == 0
    mine = jnp.stack([earlier + jnp.where(first, 0.0, got[0]), later + jnp.where(first, got[1], 0.0)])
    theirs = jnp.stack([earlier + jnp.where(first, keep[0], 0.0), later + jnp.where(first, 0.0, keep[1])])
    return mine.astype(BF16), lax.ppermute(theirs.astype(BF16), DEVICES, swap)


def body(queries, keys, values, out_grad):
    kv = keys.shape[1] // HD
    shape = (2, kv // 2, HD, HD)
    vmem = pl.BlockSpec(memory_space=pltpu.VMEM)
    anywhere = pl.BlockSpec(memory_space=pltpu.HBM)
    inputs = (queries, keys, values, out_grad)
    tokens, wide, narrow = queries.shape[0], queries.shape[1], keys.shape[1]
    keep, send = pl.pallas_call(
        states_kernel,
        out_shape=(jax.ShapeDtypeStruct(shape, BF16),) * 2,
        in_specs=[anywhere] * 4,
        out_specs=[vmem] * 2,
        scratch_shapes=[pltpu.VMEM(x.shape, BF16) for x in inputs] + [pltpu.SemaphoreType.DMA((2, kv + 1))],
        compiler_params=pltpu.CompilerParams(vmem_limit_bytes=55104 * 1024),
    )(*inputs)
    local = pl.pallas_call(
        local_kernel,
        out_shape=tuple(jax.ShapeDtypeStruct(x.shape, F32) for x in (queries, keys, values)),
        in_specs=[vmem] * 4,
        out_specs=[vmem] * 3,
        cost_estimate=pl.CostEstimate(
            flops=12 * tokens * tokens * wide, bytes_accessed=12 * tokens * wide, transcendentals=0
        ),
        compiler_params=pltpu.CompilerParams(vmem_limit_bytes=24 * MIB),
    )(*inputs)
    mine, other = carry_states(keep, send)
    return pl.pallas_call(
        finish_kernel,
        out_shape=tuple(jax.ShapeDtypeStruct(x.shape, BF16) for x in (queries, keys, values)),
        in_specs=[vmem] * 8,
        out_specs=[anywhere] * 3,
        scratch_shapes=[pltpu.VMEM((2,) + shape, BF16)]
        + [pltpu.VMEM(x.shape, BF16) for x in (queries, keys, values)]
        + [pltpu.SemaphoreType.DMA((kv + 2,))],
        compiler_params=pltpu.CompilerParams(vmem_limit_bytes=24 * MIB),
    )(keys, values, out_grad, *local, mine, other)


def solution(mesh):
    spec = P(DEVICES, None)
    return jax.shard_map(
        body, mesh=mesh, in_specs=(spec,) * 4, out_specs=(spec,) * 3, check_vma=False
    )
```

```python
import functools

import jax
import jax.numpy as jnp
from jax import lax
from jax.experimental import pallas as pl
from jax.experimental.pallas import tpu as pltpu
from jax.sharding import PartitionSpec as P

HD = 128
SEQ = "seq"
HEAD = "head"
DEVICES = (SEQ, HEAD)
LOW_ORDER = (1, 2, 3)
TOP_ORDER = (3, 2, 1)
MIB = 1024 * 1024
BF16 = jnp.bfloat16
F32 = jnp.float32

NN = (((1,), (0,)), ((), ()))
NT = (((1,), (1,)), ((), ()))
TN = (((0,), (0,)), ((), ()))


def dot(left, right, dims):
    return lax.dot_general(left, right, dims, preferred_element_type=F32)


def columns(index):
    return (slice(None), slice(index * HD, (index + 1) * HD))


def device_index():
    return lax.axis_index(SEQ) * lax.axis_size(HEAD) + lax.axis_index(HEAD)


def row_scale(tokens, shape, axis):
    positions = device_index() * tokens + lax.broadcasted_iota(jnp.int32, shape, axis)
    return 1.0 / jnp.sqrt((HD * (positions + 1)).astype(F32))


def states_kernel(q_hbm, k_hbm, v_hbm, o_hbm, keep_ref, send_ref, q_ref, k_ref, v_ref, o_ref, sems):
    tokens = q_hbm.shape[0]
    kv = k_hbm.shape[1] // HD
    width = q_hbm.shape[1] // kv
    group = width // HD
    half = kv // 2
    small = [
        pltpu.make_async_copy(k_hbm, k_ref, sems.at[0, 0]),
        pltpu.make_async_copy(v_hbm, v_ref, sems.at[1, 0]),
    ]
    large = []
    for g in range(kv):
        at = (slice(None), slice(g * width, (g + 1) * width))
        large.append(
            [
                pltpu.make_async_copy(o_hbm.at[at], o_ref.at[at], sems.at[0, 1 + g]),
                pltpu.make_async_copy(q_hbm.at[at], q_ref.at[at], sems.at[1, 1 + g]),
            ]
        )
    for copy in small:
        copy.start()
    for copies in large:
        for copy in copies:
            copy.start()
    side = side_of(device_index(), lax.axis_size(SEQ) * lax.axis_size(HEAD))
    scale = row_scale(tokens, (tokens, HD), 0)

    def put(g, kind, state):
        mine = side == g // half

        @pl.when(mine)
        def _():
            keep_ref[kind, g % half] = state

        @pl.when(jnp.logical_not(mine))
        def _():
            send_ref[kind, g % half] = state

    for copy in small:
        copy.wait()
    for g in range(kv):
        put(g, 0, dot(v_ref[columns(g)], k_ref[columns(g)], TN).astype(BF16))
    for g in range(kv):
        for copy in large[g]:
            copy.wait()
        grad = jnp.zeros((HD, HD), F32)
        for h in range(g * group, (g + 1) * group):
            scaled = (scale * o_ref[columns(h)].astype(F32)).astype(BF16)
            grad = grad + dot(scaled, q_ref[columns(h)], TN)
        put(g, 1, grad.astype(BF16))


def local_kernel(q_ref, k_ref, v_ref, o_ref, keep_ref, got_ref, qg_ref, kg_ref, vg_ref, total_ref):
    total_ref[...] = keep_ref[...].astype(F32) + got_ref[...].astype(F32)
    tokens = q_ref.shape[0]
    kv = k_ref.shape[1] // HD
    group = q_ref.shape[1] // HD // kv
    scale = row_scale(tokens, (tokens, HD), 0)
    scale_row = row_scale(tokens, (HD, tokens), 1)
    rows = lax.broadcasted_iota(jnp.int32, (tokens, tokens), 0)
    cols = lax.broadcasted_iota(jnp.int32, (tokens, tokens), 1)
    causal = rows >= cols
    causal_t = rows <= cols
    for g in range(kv):
        key = k_ref[columns(g)]
        value = v_ref[columns(g)]
        key_grad = jnp.zeros((tokens, HD), F32)
        value_grad = jnp.zeros((tokens, HD), F32)
        for h in range(g * group, (g + 1) * group):
            query = q_ref[columns(h)]
            cot = o_ref[columns(h)]
            scaled = (scale * cot.astype(F32)).astype(BF16)
            backward = jnp.where(causal, dot(scaled, value, NT), 0.0).astype(BF16)
            backward_t = jnp.where(causal_t, dot(value, scaled, NT), 0.0).astype(BF16)
            forward_t = jnp.where(causal_t, scale_row * dot(key, query, NT), 0.0).astype(BF16)
            qg_ref[columns(h)] = dot(backward, key, NN)
            key_grad = key_grad + dot(backward_t, query, NN)
            value_grad = value_grad + dot(forward_t, cot, NN)
        kg_ref[columns(g)] = key_grad
        vg_ref[columns(g)] = value_grad


def finish_kernel(
    k_ref, v_ref, o_ref, ql_ref, kl_ref, vl_ref, mine_ref, other_ref,
    qg_hbm, kg_hbm, vg_hbm, carried, qg_ref, kg_ref, vg_ref, sems,
):
    tokens = o_ref.shape[0]
    kv = k_ref.shape[1] // HD
    width = o_ref.shape[1] // kv
    group = width // HD
    half = kv // 2
    side = side_of(device_index(), lax.axis_size(SEQ) * lax.axis_size(HEAD))
    carried[side] = mine_ref[...]
    carried[1 - side] = other_ref[...]
    scale = row_scale(tokens, (tokens, HD), 0)
    copies = []
    for g in range(kv):
        prior = carried[g // half, 0, g % half]
        for h in range(g * group, (g + 1) * group):
            scaled = (scale * o_ref[columns(h)].astype(F32)).astype(BF16)
            qg_ref[columns(h)] = (ql_ref[columns(h)] + dot(scaled, prior, NN)).astype(BF16)
        at = (slice(None), slice(g * width, (g + 1) * width))
        copies.append(pltpu.make_async_copy(qg_ref.at[at], qg_hbm.at[at], sems.at[g]))
        copies[-1].start()
    for g in range(kv):
        future = carried[g // half, 1, g % half]
        key_grad = kl_ref[columns(g)] + dot(v_ref[columns(g)], future, NN)
        value_grad = vl_ref[columns(g)] + dot(k_ref[columns(g)], future, NT)
        kg_ref[columns(g)] = key_grad.astype(BF16)
        vg_ref[columns(g)] = value_grad.astype(BF16)
    copies.append(pltpu.make_async_copy(kg_ref, kg_hbm, sems.at[kv]))
    copies.append(pltpu.make_async_copy(vg_ref, vg_hbm, sems.at[kv + 1]))
    for copy in copies[-2:]:
        copy.start()
    for copy in copies:
        copy.wait()


def digits(size):
    bits = size.bit_length() - 1
    assert 1 << bits == size
    return [(low, min(2, bits - low)) for low in range(1, bits, 2)]


def side_mask(size):
    places = digits(size)
    mask = 1 | 1 << places[-1][0]
    for low, width in places[:-1]:
        mask |= ((1 << width) - 1) << low
    return mask


def side_of(index, size):
    mask = side_mask(size)
    side = index & 1
    for bit in range(1, size.bit_length()):
        if mask >> bit & 1:
            side = side ^ (index >> bit & 1)
    return side


def moved(index, size, place, step, last):
    low, width = place
    base = (1 << width) - 1
    digit = index >> low & base
    new = (digit + step & base) if last else digit ^ step
    other = index ^ (digit ^ new) << low
    return other ^ side_of(other, size) ^ side_of(index, size)


def carry_states(keep, send, local_terms):
    size = lax.axis_size(SEQ) * lax.axis_size(HEAD)
    index = device_index()
    swap = [(i, i ^ 1) for i in range(size)]
    got = lax.ppermute(send, DEVICES, swap)
    *local, total = local_terms(keep, got)
    keep = keep.astype(F32)
    got = got.astype(F32)
    message = (keep + got).astype(BF16)
    earlier = jnp.zeros_like(total[0])
    later = jnp.zeros_like(total[1])
    places = digits(size)
    for place in places[:-1]:
        for step in [step for step in LOW_ORDER if step < 1 << place[1]]:
            arrived = lax.ppermute(
                message, DEVICES, [(i, moved(i, size, place, step, False)) for i in range(size)]
            ).astype(F32)
            lower = index < (index ^ step << place[0])
            earlier = earlier + jnp.where(lower, 0.0, arrived[0])
            later = later + jnp.where(lower, arrived[1], 0.0)
            total = total + arrived
        message = total.astype(BF16)
    place = places[-1]
    count = 1 << place[1]
    digit = index >> place[0] & count - 1
    steps = [step for step in TOP_ORDER if step < count]
    messages = [jnp.where(digit + step < count, message[0], message[1]) for step in steps]
    messages = lax.optimization_barrier(tuple(messages))
    for step, message in zip(steps, messages):
        arrived = lax.ppermute(
            message, DEVICES, [(i, moved(i, size, place, step, True)) for i in range(size)]
        ).astype(F32)
        before = digit >= step
        earlier = earlier + jnp.where(before, arrived, 0.0)
        later = later + jnp.where(before, 0.0, arrived)
    first = index & 1 == 0
    mine = jnp.stack([earlier + jnp.where(first, 0.0, got[0]), later + jnp.where(first, got[1], 0.0)])
    theirs = jnp.stack([earlier + jnp.where(first, keep[0], 0.0), later + jnp.where(first, 0.0, keep[1])])
    return local, mine.astype(BF16), lax.ppermute(theirs.astype(BF16), DEVICES, swap)


def body(queries, keys, values, out_grad):
    kv = keys.shape[1] // HD
    shape = (2, kv // 2, HD, HD)
    vmem = pl.BlockSpec(memory_space=pltpu.VMEM)
    anywhere = pl.BlockSpec(memory_space=pltpu.HBM)
    inputs = (queries, keys, values, out_grad)
    tokens, wide, narrow = queries.shape[0], queries.shape[1], keys.shape[1]
    keep, send = pl.pallas_call(
        states_kernel,
        out_shape=(jax.ShapeDtypeStruct(shape, BF16),) * 2,
        in_specs=[anywhere] * 4,
        out_specs=[vmem] * 2,
        scratch_shapes=[pltpu.VMEM(x.shape, BF16) for x in inputs] + [pltpu.SemaphoreType.DMA((2, kv + 1))],
        compiler_params=pltpu.CompilerParams(vmem_limit_bytes=55104 * 1024),
    )(*inputs)
    local_terms = pl.pallas_call(
        local_kernel,
        out_shape=tuple(jax.ShapeDtypeStruct(x.shape, F32) for x in (queries, keys, values, keep)),
        in_specs=[vmem] * 6,
        out_specs=[vmem] * 4,
        cost_estimate=pl.CostEstimate(
            flops=12 * tokens * tokens * wide, bytes_accessed=12 * tokens * wide, transcendentals=0
        ),
        compiler_params=pltpu.CompilerParams(vmem_limit_bytes=24 * MIB),
    )
    local, mine, other = carry_states(keep, send, functools.partial(local_terms, *inputs))
    return pl.pallas_call(
        finish_kernel,
        out_shape=tuple(jax.ShapeDtypeStruct(x.shape, BF16) for x in (queries, keys, values)),
        in_specs=[vmem] * 8,
        out_specs=[anywhere] * 3,
        scratch_shapes=[pltpu.VMEM((2,) + shape, BF16)]
        + [pltpu.VMEM(x.shape, BF16) for x in (queries, keys, values)]
        + [pltpu.SemaphoreType.DMA((kv + 2,))],
        compiler_params=pltpu.CompilerParams(vmem_limit_bytes=24 * MIB),
    )(keys, values, out_grad, *local, mine, other)


def solution(mesh):
    spec = P(DEVICES, None)
    return jax.shard_map(
        body, mesh=mesh, in_specs=(spec,) * 4, out_specs=(spec,) * 3, check_vma=False
    )
```

```python
import functools

import jax
import jax.numpy as jnp
from jax import lax
from jax.experimental import pallas as pl
from jax.experimental.pallas import tpu as pltpu
from jax.sharding import PartitionSpec as P

HD = 128
SEQ = "seq"
HEAD = "head"
DEVICES = (SEQ, HEAD)
LOW_MOVES = ((1, 0, 3, 2), (2, 3, 0, 1), (3, 2, 1, 0))
TOP_MOVES = ((3, 0, 1, 2), (2, 3, 0, 1), (1, 2, 3, 0))
LOW_ODD = (0, 1, 1, 0)
TOP_ODD = (0, 1, 0, 1)
MIB = 1024 * 1024
BF16 = jnp.bfloat16
F32 = jnp.float32

NN = (((1,), (0,)), ((), ()))
NT = (((1,), (1,)), ((), ()))
TN = (((0,), (0,)), ((), ()))


def dot(left, right, dims):
    return lax.dot_general(left, right, dims, preferred_element_type=F32)


def columns(index):
    return (slice(None), slice(index * HD, (index + 1) * HD))


def device_index():
    return lax.axis_index(SEQ) * lax.axis_size(HEAD) + lax.axis_index(HEAD)


def row_scale(tokens, shape, axis):
    positions = device_index() * tokens + lax.broadcasted_iota(jnp.int32, shape, axis)
    return 1.0 / jnp.sqrt((HD * (positions + 1)).astype(F32))


def states_kernel(q_hbm, k_hbm, v_hbm, o_hbm, keep_ref, send_ref, q_ref, k_ref, v_ref, o_ref, sems):
    tokens = q_hbm.shape[0]
    kv = k_hbm.shape[1] // HD
    group = q_hbm.shape[1] // HD // kv
    half = kv // 2
    arrivals = [
        pltpu.make_async_copy(source, place, sems.at[i])
        for i, (source, place) in enumerate([(k_hbm, k_ref), (v_hbm, v_ref), (o_hbm, o_ref), (q_hbm, q_ref)])
    ]
    for copy in arrivals:
        copy.start(priority=1)
    side = side_of(device_index(), lax.axis_size(SEQ) * lax.axis_size(HEAD))
    scale = row_scale(tokens, (tokens, HD), 0)

    def put(g, kind, state):
        mine = side == g // half

        @pl.when(mine)
        def _():
            keep_ref[kind, g % half] = state

        @pl.when(jnp.logical_not(mine))
        def _():
            send_ref[kind, g % half] = state

    arrivals[0].wait()
    arrivals[1].wait()
    for g in range(kv):
        put(g, 0, dot(v_ref[columns(g)], k_ref[columns(g)], TN).astype(BF16))
    arrivals[2].wait()
    scaled = [(scale * o_ref[columns(h)].astype(F32)).astype(BF16) for h in range(kv * group)]
    arrivals[3].wait()
    for g in range(kv):
        grad = jnp.zeros((HD, HD), F32)
        for h in range(g * group, (g + 1) * group):
            grad = grad + dot(scaled[h], q_ref[columns(h)], TN)
        put(g, 1, grad.astype(BF16))


def local_kernel(q_ref, k_ref, v_ref, o_ref, keep_ref, got_ref, qg_ref, kg_ref, vg_ref, total_ref):
    total_ref[...] = keep_ref[...].astype(F32) + got_ref[...].astype(F32)
    tokens = q_ref.shape[0]
    kv = k_ref.shape[1] // HD
    group = q_ref.shape[1] // HD // kv
    scale = row_scale(tokens, (tokens, HD), 0)
    scale_row = row_scale(tokens, (HD, tokens), 1)
    rows = lax.broadcasted_iota(jnp.int32, (tokens, tokens), 0)
    cols = lax.broadcasted_iota(jnp.int32, (tokens, tokens), 1)
    causal = rows >= cols
    causal_t = rows <= cols
    for g in range(kv):
        key = k_ref[columns(g)]
        value = v_ref[columns(g)]
        key_grad = jnp.zeros((tokens, HD), F32)
        value_grad = jnp.zeros((tokens, HD), F32)
        for h in range(g * group, (g + 1) * group):
            query = q_ref[columns(h)]
            cot = o_ref[columns(h)]
            scaled = (scale * cot.astype(F32)).astype(BF16)
            backward = jnp.where(causal, dot(scaled, value, NT), 0.0).astype(BF16)
            backward_t = jnp.where(causal_t, dot(value, scaled, NT), 0.0).astype(BF16)
            forward_t = jnp.where(causal_t, scale_row * dot(key, query, NT), 0.0).astype(BF16)
            qg_ref[columns(h)] = dot(backward, key, NN)
            key_grad = key_grad + dot(backward_t, query, NN)
            value_grad = value_grad + dot(forward_t, cot, NN)
        kg_ref[columns(g)] = key_grad
        vg_ref[columns(g)] = value_grad


def finish_kernel(mine, k_ref, v_ref, o_ref, ql_ref, kl_ref, vl_ref, state_ref, *refs):
    qg_hbm, kg_hbm, vg_hbm, qg_ref, kg_ref, vg_ref, sems = refs[-7:]
    tokens = o_ref.shape[0]
    kv = k_ref.shape[1] // HD
    width = o_ref.shape[1] // kv
    group = width // HD
    half = kv // 2
    side = side_of(device_index(), lax.axis_size(SEQ) * lax.axis_size(HEAD))
    scale = row_scale(tokens, (tokens, HD), 0)

    def finish(part):
        copies = []

        def send(ref, hbm, size):
            at = (slice(None), slice(part * half * size, (part + 1) * half * size))
            copies.append(pltpu.make_async_copy(ref.at[at], hbm.at[at], sems.at[len(copies)]))
            copies[-1].start()

        for g in range(part * half, (part + 1) * half):
            prior = state_ref[0, g % half]
            for h in range(g * group, (g + 1) * group):
                scaled = (scale * o_ref[columns(h)].astype(F32)).astype(BF16)
                qg_ref[columns(h)] = (ql_ref[columns(h)] + dot(scaled, prior, NN)).astype(BF16)
        send(qg_ref, qg_hbm, width)
        for g in range(part * half, (part + 1) * half):
            future = state_ref[1, g % half]
            key_grad = kl_ref[columns(g)] + dot(v_ref[columns(g)], future, NN)
            value_grad = vl_ref[columns(g)] + dot(k_ref[columns(g)], future, NT)
            kg_ref[columns(g)] = key_grad.astype(BF16)
            vg_ref[columns(g)] = value_grad.astype(BF16)
        send(kg_ref, kg_hbm, HD)
        send(vg_ref, vg_hbm, HD)
        for copy in copies:
            copy.wait()

    for part in range(2):
        pl.when(side == (part if mine else 1 - part))(functools.partial(finish, part))


def digits(size):
    bits = size.bit_length() - 1
    assert 1 << bits == size
    return [(low, min(2, bits - low)) for low in range(1, bits, 2)]


def tables(size):
    found = []
    for low, width in digits(size):
        moves, odd = (LOW_MOVES, LOW_ODD) if low + width < size.bit_length() - 1 else (TOP_MOVES, TOP_ODD)
        found.append((low, moves, odd) if width == 2 else (low, ((1, 0),), (0, 1)))
    return found


def side_of(index, size):
    side = index & 1
    for low, moves, odd in tables(size):
        digit = index >> low & len(odd) - 1
        for place in range(len(odd)):
            if odd[place]:
                side = side ^ (digit == place)
    return side


def target(index, size, low, move):
    digit = index >> low & len(move) - 1
    other = index ^ (digit ^ move[digit]) << low
    return other ^ side_of(other, size) ^ side_of(index, size)


def place_among(digit, places):
    return sum(jnp.where(digit == place, other, 0) for place, other in enumerate(places))


def carry_states(keep, send, local_terms):
    size = lax.axis_size(SEQ) * lax.axis_size(HEAD)
    index = device_index()
    swap = [(i, i ^ 1) for i in range(size)]
    got = lax.ppermute(send, DEVICES, swap)
    *local, total = local_terms(keep, got)
    keep = keep.astype(F32)
    got = got.astype(F32)
    message = (keep + got).astype(BF16)
    earlier = jnp.zeros_like(total[0])
    later = jnp.zeros_like(total[1])
    *low_rounds, top_round = tables(size)
    for low, moves, _ in low_rounds:
        digit = index >> low & len(moves)
        for move in moves:
            arrived = lax.ppermute(
                message, DEVICES, [(i, target(i, size, low, move)) for i in range(size)]
            ).astype(F32)
            before = place_among(digit, [move.index(place) for place in range(len(move))]) < digit
            earlier = earlier + jnp.where(before, arrived[0], 0.0)
            later = later + jnp.where(before, 0.0, arrived[1])
            total = total + arrived
        message = total.astype(BF16)
    low, moves, _ = top_round
    digit = index >> low & len(moves)
    messages = [jnp.where(place_among(digit, move) > digit, message[0], message[1]) for move in moves]
    messages = lax.optimization_barrier(tuple(messages))
    for move, message in zip(moves, messages):
        arrived = lax.ppermute(
            message, DEVICES, [(i, target(i, size, low, move)) for i in range(size)]
        ).astype(F32)
        before = place_among(digit, [move.index(place) for place in range(len(move))]) < digit
        earlier = earlier + jnp.where(before, arrived, 0.0)
        later = later + jnp.where(before, 0.0, arrived)
    first = index & 1 == 0
    mine = jnp.stack([earlier + jnp.where(first, 0.0, got[0]), later + jnp.where(first, got[1], 0.0)])
    theirs = jnp.stack([earlier + jnp.where(first, keep[0], 0.0), later + jnp.where(first, 0.0, keep[1])])
    return local, mine.astype(BF16), lax.ppermute(theirs.astype(BF16), DEVICES, swap)


def body(queries, keys, values, out_grad):
    kv = keys.shape[1] // HD
    shape = (2, kv // 2, HD, HD)
    vmem = pl.BlockSpec(memory_space=pltpu.VMEM)
    anywhere = pl.BlockSpec(memory_space=pltpu.HBM)
    inputs = (queries, keys, values, out_grad)
    tokens, wide, narrow = queries.shape[0], queries.shape[1], keys.shape[1]
    keep, send = pl.pallas_call(
        states_kernel,
        out_shape=(jax.ShapeDtypeStruct(shape, BF16),) * 2,
        in_specs=[anywhere] * 4,
        out_specs=[vmem] * 2,
        scratch_shapes=[pltpu.VMEM(x.shape, BF16) for x in inputs] + [pltpu.SemaphoreType.DMA((4,))],
        compiler_params=pltpu.CompilerParams(vmem_limit_bytes=55104 * 1024),
    )(*inputs)
    local_terms = pl.pallas_call(
        local_kernel,
        out_shape=tuple(jax.ShapeDtypeStruct(x.shape, F32) for x in (queries, keys, values, keep)),
        in_specs=[vmem] * 6,
        out_specs=[vmem] * 4,
        cost_estimate=pl.CostEstimate(
            flops=12 * tokens * tokens * wide, bytes_accessed=12 * tokens * wide, transcendentals=0
        ),
        compiler_params=pltpu.CompilerParams(vmem_limit_bytes=24 * MIB),
    )
    local, mine, other = carry_states(keep, send, functools.partial(local_terms, *inputs))

    def finish(mine, state, *written):
        return pl.pallas_call(
            functools.partial(finish_kernel, mine),
            out_shape=tuple(jax.ShapeDtypeStruct(x.shape, BF16) for x in (queries, keys, values)),
            in_specs=[vmem] * 7 + [anywhere] * len(written),
            out_specs=[anywhere] * 3,
            scratch_shapes=[pltpu.VMEM(x.shape, BF16) for x in (queries, keys, values)]
            + [pltpu.SemaphoreType.DMA((3,))],
            input_output_aliases={7 + i: i for i in range(len(written))},
            cost_estimate=pl.CostEstimate(
                flops=4 * tokens * HD * wide, bytes_accessed=4 * tokens * wide, transcendentals=0
            ),
            compiler_params=pltpu.CompilerParams(vmem_limit_bytes=24 * MIB),
        )(keys, values, out_grad, *local, state, *written)

    return finish(False, other, *finish(True, mine))


def solution(mesh):
    spec = P(DEVICES, None)
    return jax.shard_map(
        body, mesh=mesh, in_specs=(spec,) * 4, out_specs=(spec,) * 3, check_vma=False
    )
```

```python
import functools

import jax
import jax.numpy as jnp
from jax import lax
from jax.experimental import pallas as pl
from jax.experimental.pallas import tpu as pltpu
from jax.sharding import PartitionSpec as P

HD = 128
SEQ = "seq"
HEAD = "head"
DEVICES = (SEQ, HEAD)
LOW_MOVES = ((1, 0, 3, 2), (2, 3, 0, 1), (3, 2, 1, 0))
TOP_MOVES = ((3, 0, 1, 2), (2, 3, 0, 1), (1, 2, 3, 0))
LOW_ODD = (0, 1, 1, 0)
TOP_ODD = (0, 1, 0, 1)
MIB = 1024 * 1024
BF16 = jnp.bfloat16
F32 = jnp.float32

NN = (((1,), (0,)), ((), ()))
NT = (((1,), (1,)), ((), ()))
TN = (((0,), (0,)), ((), ()))


def dot(left, right, dims):
    return lax.dot_general(left, right, dims, preferred_element_type=F32)


def columns(index):
    return (slice(None), slice(index * HD, (index + 1) * HD))


def device_index():
    return lax.axis_index(SEQ) * lax.axis_size(HEAD) + lax.axis_index(HEAD)


def row_scale(tokens, shape, axis):
    positions = device_index() * tokens + lax.broadcasted_iota(jnp.int32, shape, axis)
    return 1.0 / jnp.sqrt((HD * (positions + 1)).astype(F32))


def half_states(k_ref, v_ref, o_ref, q_ref, out_ref):
    tokens = q_ref.shape[0]
    half = k_ref.shape[1] // HD
    group = q_ref.shape[1] // k_ref.shape[1]
    scale = row_scale(tokens, (tokens, HD), 0)
    for g in range(half):
        out_ref[0, g] = dot(v_ref[columns(g)], k_ref[columns(g)], TN).astype(BF16)
    for g in range(half):
        grad = jnp.zeros((HD, HD), F32)
        for h in range(g * group, (g + 1) * group):
            scaled = (scale * o_ref[columns(h)].astype(F32)).astype(BF16)
            grad = grad + dot(scaled, q_ref[columns(h)], TN)
        out_ref[1, g] = grad.astype(BF16)


def half_columns(ref, side):
    width = ref.shape[1] // 2
    return ref.at[:, pl.ds(pl.multiple_of(side * width, HD), width)]


def send_kernel(k_hbm, v_hbm, o_hbm, q_hbm, out_ref, k_ref, v_ref, o_ref, q_ref, sems):
    side = 1 - side_of(device_index(), lax.axis_size(SEQ) * lax.axis_size(HEAD))
    copies = [
        pltpu.make_async_copy(half_columns(source, side), place, sems.at[i])
        for i, (source, place) in enumerate([(k_hbm, k_ref), (v_hbm, v_ref), (o_hbm, o_ref), (q_hbm, q_ref)])
    ]
    for copy in copies:
        copy.start(priority=1)
    for copy in copies:
        copy.wait()
    half_states(k_ref, v_ref, o_ref, q_ref, out_ref)


def keep_kernel(k_ref, v_ref, o_ref, q_ref, out_ref):
    side = side_of(device_index(), lax.axis_size(SEQ) * lax.axis_size(HEAD))
    half_states(*[half_columns(ref, side) for ref in (k_ref, v_ref, o_ref, q_ref)], out_ref)


def local_kernel(q_ref, k_ref, v_ref, o_ref, keep_ref, got_ref, qg_ref, kg_ref, vg_ref, total_ref):
    total_ref[...] = keep_ref[...].astype(F32) + got_ref[...].astype(F32)
    tokens = q_ref.shape[0]
    kv = k_ref.shape[1] // HD
    group = q_ref.shape[1] // HD // kv
    scale = row_scale(tokens, (tokens, HD), 0)
    scale_row = row_scale(tokens, (HD, tokens), 1)
    rows = lax.broadcasted_iota(jnp.int32, (tokens, tokens), 0)
    cols = lax.broadcasted_iota(jnp.int32, (tokens, tokens), 1)
    causal = rows >= cols
    causal_t = rows <= cols
    for g in range(kv):
        key = k_ref[columns(g)]
        value = v_ref[columns(g)]
        key_grad = jnp.zeros((tokens, HD), F32)
        value_grad = jnp.zeros((tokens, HD), F32)
        for h in range(g * group, (g + 1) * group):
            query = q_ref[columns(h)]
            cot = o_ref[columns(h)]
            scaled = (scale * cot.astype(F32)).astype(BF16)
            backward = jnp.where(causal, dot(scaled, value, NT), 0.0).astype(BF16)
            backward_t = jnp.where(causal_t, dot(value, scaled, NT), 0.0).astype(BF16)
            forward_t = jnp.where(causal_t, scale_row * dot(key, query, NT), 0.0).astype(BF16)
            qg_ref[columns(h)] = dot(backward, key, NN)
            key_grad = key_grad + dot(backward_t, query, NN)
            value_grad = value_grad + dot(forward_t, cot, NN)
        kg_ref[columns(g)] = key_grad
        vg_ref[columns(g)] = value_grad


def finish_kernel(mine, k_ref, v_ref, o_ref, ql_ref, kl_ref, vl_ref, state_ref, *refs):
    qg_hbm, kg_hbm, vg_hbm, qg_ref, kg_ref, vg_ref, sems = refs[-7:]
    tokens = o_ref.shape[0]
    kv = k_ref.shape[1] // HD
    width = o_ref.shape[1] // kv
    group = width // HD
    half = kv // 2
    side = side_of(device_index(), lax.axis_size(SEQ) * lax.axis_size(HEAD))
    scale = row_scale(tokens, (tokens, HD), 0)

    def finish(part):
        copies = []

        def send(ref, hbm, size):
            at = (slice(None), slice(part * half * size, (part + 1) * half * size))
            copies.append(pltpu.make_async_copy(ref.at[at], hbm.at[at], sems.at[len(copies)]))
            copies[-1].start()

        for g in range(part * half, (part + 1) * half):
            prior = state_ref[0, g % half]
            for h in range(g * group, (g + 1) * group):
                scaled = (scale * o_ref[columns(h)].astype(F32)).astype(BF16)
                qg_ref[columns(h)] = (ql_ref[columns(h)] + dot(scaled, prior, NN)).astype(BF16)
        send(qg_ref, qg_hbm, width)
        for g in range(part * half, (part + 1) * half):
            future = state_ref[1, g % half]
            key_grad = kl_ref[columns(g)] + dot(v_ref[columns(g)], future, NN)
            value_grad = vl_ref[columns(g)] + dot(k_ref[columns(g)], future, NT)
            kg_ref[columns(g)] = key_grad.astype(BF16)
            vg_ref[columns(g)] = value_grad.astype(BF16)
        send(kg_ref, kg_hbm, HD)
        send(vg_ref, vg_hbm, HD)
        for copy in copies:
            copy.wait()

    for part in range(2):
        pl.when(side == (part if mine else 1 - part))(functools.partial(finish, part))


def digits(size):
    bits = size.bit_length() - 1
    assert 1 << bits == size
    return [(low, min(2, bits - low)) for low in range(1, bits, 2)]


def tables(size):
    found = []
    for low, width in digits(size):
        moves, odd = (LOW_MOVES, LOW_ODD) if low + width < size.bit_length() - 1 else (TOP_MOVES, TOP_ODD)
        found.append((low, moves, odd) if width == 2 else (low, ((1, 0),), (0, 1)))
    return found


def side_of(index, size):
    side = index & 1
    for low, moves, odd in tables(size):
        digit = index >> low & len(odd) - 1
        for place in range(len(odd)):
            if odd[place]:
                side = side ^ (digit == place)
    return side


def target(index, size, low, move):
    digit = index >> low & len(move) - 1
    other = index ^ (digit ^ move[digit]) << low
    return other ^ side_of(other, size) ^ side_of(index, size)


def place_among(digit, places):
    return sum(jnp.where(digit == place, other, 0) for place, other in enumerate(places))


def carry_states(keep, send, local_terms):
    size = lax.axis_size(SEQ) * lax.axis_size(HEAD)
    index = device_index()
    swap = [(i, i ^ 1) for i in range(size)]
    got = lax.ppermute(send, DEVICES, swap)
    keep = keep()
    *local, total = local_terms(keep, got)
    keep = keep.astype(F32)
    got = got.astype(F32)
    message = (keep + got).astype(BF16)
    earlier = jnp.zeros_like(total[0])
    later = jnp.zeros_like(total[1])
    *low_rounds, top_round = tables(size)
    for low, moves, _ in low_rounds:
        digit = index >> low & len(moves)
        for move in moves:
            arrived = lax.ppermute(
                message, DEVICES, [(i, target(i, size, low, move)) for i in range(size)]
            ).astype(F32)
            before = place_among(digit, [move.index(place) for place in range(len(move))]) < digit
            earlier = earlier + jnp.where(before, arrived[0], 0.0)
            later = later + jnp.where(before, 0.0, arrived[1])
            total = total + arrived
        message = total.astype(BF16)
    low, moves, _ = top_round
    digit = index >> low & len(moves)
    messages = [jnp.where(place_among(digit, move) > digit, message[0], message[1]) for move in moves]
    messages = lax.optimization_barrier(tuple(messages))
    for move, message in zip(moves, messages):
        arrived = lax.ppermute(
            message, DEVICES, [(i, target(i, size, low, move)) for i in range(size)]
        ).astype(F32)
        before = place_among(digit, [move.index(place) for place in range(len(move))]) < digit
        earlier = earlier + jnp.where(before, arrived, 0.0)
        later = later + jnp.where(before, 0.0, arrived)
    first = index & 1 == 0
    mine = jnp.stack([earlier + jnp.where(first, 0.0, got[0]), later + jnp.where(first, got[1], 0.0)])
    theirs = jnp.stack([earlier + jnp.where(first, keep[0], 0.0), later + jnp.where(first, 0.0, keep[1])])
    return local, mine.astype(BF16), lax.ppermute(theirs.astype(BF16), DEVICES, swap)


def body(queries, keys, values, out_grad):
    kv = keys.shape[1] // HD
    shape = (2, kv // 2, HD, HD)
    vmem = pl.BlockSpec(memory_space=pltpu.VMEM)
    anywhere = pl.BlockSpec(memory_space=pltpu.HBM)
    inputs = (queries, keys, values, out_grad)
    tokens, wide, narrow = queries.shape[0], queries.shape[1], keys.shape[1]
    ordered = (keys, values, out_grad, queries)
    halves = [pltpu.VMEM((x.shape[0], x.shape[1] // 2), BF16) for x in ordered]
    send = pl.pallas_call(
        send_kernel,
        out_shape=jax.ShapeDtypeStruct(shape, BF16),
        in_specs=[anywhere] * 4,
        out_specs=vmem,
        scratch_shapes=halves + [pltpu.SemaphoreType.DMA((4,))],
        compiler_params=pltpu.CompilerParams(vmem_limit_bytes=55144 * 1024),
    )(*ordered)

    def keep():
        return pl.pallas_call(
            keep_kernel,
            out_shape=jax.ShapeDtypeStruct(shape, BF16),
            in_specs=[vmem] * 4,
            out_specs=vmem,
            cost_estimate=pl.CostEstimate(
                flops=2 * tokens * HD * wide, bytes_accessed=4 * tokens * wide, transcendentals=0
            ),
            compiler_params=pltpu.CompilerParams(vmem_limit_bytes=24 * MIB),
        )(*ordered)

    local_terms = pl.pallas_call(
        local_kernel,
        out_shape=tuple(jax.ShapeDtypeStruct(x.shape, F32) for x in (queries, keys, values, send)),
        in_specs=[vmem] * 6,
        out_specs=[vmem] * 4,
        cost_estimate=pl.CostEstimate(
            flops=12 * tokens * tokens * wide, bytes_accessed=12 * tokens * wide, transcendentals=0
        ),
        compiler_params=pltpu.CompilerParams(vmem_limit_bytes=24 * MIB),
    )
    local, mine, other = carry_states(keep, send, functools.partial(local_terms, *inputs))

    def finish(mine, state, *written):
        return pl.pallas_call(
            functools.partial(finish_kernel, mine),
            out_shape=tuple(jax.ShapeDtypeStruct(x.shape, BF16) for x in (queries, keys, values)),
            in_specs=[vmem] * 7 + [anywhere] * len(written),
            out_specs=[anywhere] * 3,
            scratch_shapes=[pltpu.VMEM(x.shape, BF16) for x in (queries, keys, values)]
            + [pltpu.SemaphoreType.DMA((3,))],
            input_output_aliases={7 + i: i for i in range(len(written))},
            cost_estimate=pl.CostEstimate(
                flops=4 * tokens * HD * wide, bytes_accessed=4 * tokens * wide, transcendentals=0
            ),
            compiler_params=pltpu.CompilerParams(vmem_limit_bytes=24 * MIB),
        )(keys, values, out_grad, *local, state, *written)

    return finish(False, other, *finish(True, mine))


def solution(mesh):
    spec = P(DEVICES, None)
    return jax.shard_map(
        body, mesh=mesh, in_specs=(spec,) * 4, out_specs=(spec,) * 3, check_vma=False
    )
```

```python
import functools

import jax
import jax.numpy as jnp
from jax import lax
from jax.experimental import pallas as pl
from jax.experimental.pallas import tpu as pltpu
from jax.sharding import PartitionSpec as P

HD = 128
SEQ = "seq"
HEAD = "head"
DEVICES = (SEQ, HEAD)
LOW_MOVES = ((1, 0, 3, 2), (2, 3, 0, 1), (3, 2, 1, 0))
TOP_MOVES = ((3, 0, 1, 2), (2, 3, 0, 1), (1, 2, 3, 0))
LOW_ODD = (0, 1, 1, 0)
TOP_ODD = (0, 1, 0, 1)
MIB = 1024 * 1024
BF16 = jnp.bfloat16
F32 = jnp.float32

NN = (((1,), (0,)), ((), ()))
NT = (((1,), (1,)), ((), ()))
TN = (((0,), (0,)), ((), ()))


def dot(left, right, dims):
    return lax.dot_general(left, right, dims, preferred_element_type=F32)


def columns(index):
    return (slice(None), slice(index * HD, (index + 1) * HD))


def device_index():
    return lax.axis_index(SEQ) * lax.axis_size(HEAD) + lax.axis_index(HEAD)


def row_scale(tokens, shape, axis):
    positions = device_index() * tokens + lax.broadcasted_iota(jnp.int32, shape, axis)
    return 1.0 / jnp.sqrt((HD * (positions + 1)).astype(F32))


def half_states(k_ref, v_ref, o_ref, q_ref, out_ref, copies=()):
    tokens = q_ref.shape[0]
    half = k_ref.shape[1] // HD
    group = q_ref.shape[1] // k_ref.shape[1]
    scale = row_scale(tokens, (tokens, HD), 0)
    for copy in copies[:2]:
        copy.wait()
    for g in range(half):
        out_ref[0, g] = dot(v_ref[columns(g)], k_ref[columns(g)], TN).astype(BF16)
    for copy in copies[2:]:
        copy.wait()
    for g in range(half):
        grad = jnp.zeros((HD, HD), F32)
        for h in range(g * group, (g + 1) * group):
            scaled = (scale * o_ref[columns(h)].astype(F32)).astype(BF16)
            grad = grad + dot(scaled, q_ref[columns(h)], TN)
        out_ref[1, g] = grad.astype(BF16)


def half_columns(ref, side):
    width = ref.shape[1] // 2
    return ref.at[:, pl.ds(pl.multiple_of(side * width, HD), width)]


def send_kernel(k_hbm, v_hbm, o_hbm, q_hbm, out_ref, k_ref, v_ref, o_ref, q_ref, sems):
    side = 1 - side_of(device_index(), lax.axis_size(SEQ) * lax.axis_size(HEAD))
    copies = [
        pltpu.make_async_copy(half_columns(source, side), place, sems.at[i])
        for i, (source, place) in enumerate([(k_hbm, k_ref), (v_hbm, v_ref), (o_hbm, o_ref), (q_hbm, q_ref)])
    ]
    for copy in copies:
        copy.start(priority=1)
    half_states(k_ref, v_ref, o_ref, q_ref, out_ref, copies)


def keep_kernel(k_ref, v_ref, o_ref, q_ref, out_ref):
    side = side_of(device_index(), lax.axis_size(SEQ) * lax.axis_size(HEAD))
    half_states(*[half_columns(ref, side) for ref in (k_ref, v_ref, o_ref, q_ref)], out_ref)


def local_kernel(
    q_ref, k_ref, v_ref, o_ref, keep_ref, got_ref, qg_ref, kg_ref, vg_ref, scaled_ref, total_ref
):
    total_ref[...] = keep_ref[...].astype(F32) + got_ref[...].astype(F32)
    tokens = q_ref.shape[0]
    kv = k_ref.shape[1] // HD
    group = q_ref.shape[1] // HD // kv
    scale = row_scale(tokens, (tokens, HD), 0)
    scale_row = row_scale(tokens, (HD, tokens), 1)
    rows = lax.broadcasted_iota(jnp.int32, (tokens, tokens), 0)
    cols = lax.broadcasted_iota(jnp.int32, (tokens, tokens), 1)
    causal = rows >= cols
    causal_t = rows <= cols
    for g in range(kv):
        key = k_ref[columns(g)]
        value = v_ref[columns(g)]
        key_grad = jnp.zeros((tokens, HD), F32)
        value_grad = jnp.zeros((tokens, HD), F32)
        for h in range(g * group, (g + 1) * group):
            query = q_ref[columns(h)]
            cot = o_ref[columns(h)]
            scaled = (scale * cot.astype(F32)).astype(BF16)
            scaled_ref[columns(h)] = scaled
            backward = jnp.where(causal, dot(scaled, value, NT), 0.0).astype(BF16)
            backward_t = jnp.where(causal_t, dot(value, scaled, NT), 0.0).astype(BF16)
            forward_t = jnp.where(causal_t, scale_row * dot(key, query, NT), 0.0).astype(BF16)
            qg_ref[columns(h)] = dot(backward, key, NN)
            key_grad = key_grad + dot(backward_t, query, NN)
            value_grad = value_grad + dot(forward_t, cot, NN)
        kg_ref[columns(g)] = key_grad
        vg_ref[columns(g)] = value_grad


def finish_kernel(mine, k_ref, v_ref, scaled_ref, ql_ref, kl_ref, vl_ref, state_ref, *refs):
    qg_hbm, kg_hbm, vg_hbm, qg_ref, kg_ref, vg_ref, sems = refs[-7:]
    tokens = scaled_ref.shape[0]
    kv = k_ref.shape[1] // HD
    width = scaled_ref.shape[1] // kv
    group = width // HD
    half = kv // 2
    side = side_of(device_index(), lax.axis_size(SEQ) * lax.axis_size(HEAD))

    def finish(part):
        copies = []

        def send(ref, hbm, low, size):
            at = (slice(None), slice(low, low + size))
            copies.append(pltpu.make_async_copy(ref.at[at], hbm.at[at], sems.at[len(copies)]))
            copies[-1].start()

        for g in range(part * half, (part + 1) * half):
            prior = state_ref[0, g % half]
            for h in range(g * group, (g + 1) * group):
                scaled = scaled_ref[columns(h)]
                qg_ref[columns(h)] = (ql_ref[columns(h)] + dot(scaled, prior, NN)).astype(BF16)
        send(qg_ref, qg_hbm, part * half * width, half * width)
        for g in range(part * half, (part + 1) * half):
            future = state_ref[1, g % half]
            key_grad = kl_ref[columns(g)] + dot(v_ref[columns(g)], future, NN)
            value_grad = vl_ref[columns(g)] + dot(k_ref[columns(g)], future, NT)
            kg_ref[columns(g)] = key_grad.astype(BF16)
            vg_ref[columns(g)] = value_grad.astype(BF16)
        send(kg_ref, kg_hbm, part * half * HD, half * HD)
        send(vg_ref, vg_hbm, part * half * HD, half * HD)
        for copy in copies:
            copy.wait()

    for part in range(2):
        pl.when(side == (part if mine else 1 - part))(functools.partial(finish, part))


def digits(size):
    bits = size.bit_length() - 1
    assert 1 << bits == size
    return [(low, min(2, bits - low)) for low in range(1, bits, 2)]


def tables(size):
    found = []
    for low, width in digits(size):
        moves, odd = (LOW_MOVES, LOW_ODD) if low + width < size.bit_length() - 1 else (TOP_MOVES, TOP_ODD)
        found.append((low, moves, odd) if width == 2 else (low, ((1, 0),), (0, 1)))
    return found


def side_of(index, size):
    side = index & 1
    for low, moves, odd in tables(size):
        digit = index >> low & len(odd) - 1
        for place in range(len(odd)):
            if odd[place]:
                side = side ^ (digit == place)
    return side


def target(index, size, low, move):
    digit = index >> low & len(move) - 1
    other = index ^ (digit ^ move[digit]) << low
    return other ^ side_of(other, size) ^ side_of(index, size)


def place_among(digit, places):
    return sum(jnp.where(digit == place, other, 0) for place, other in enumerate(places))


def carry_states(keep, send, local_terms):
    size = lax.axis_size(SEQ) * lax.axis_size(HEAD)
    index = device_index()
    swap = [(i, i ^ 1) for i in range(size)]
    got = lax.ppermute(send, DEVICES, swap)
    keep = keep()
    *local, total = local_terms(keep, got)
    keep = keep.astype(F32)
    got = got.astype(F32)
    message = (keep + got).astype(BF16)
    earlier = jnp.zeros_like(total[0])
    later = jnp.zeros_like(total[1])
    *low_rounds, top_round = tables(size)
    for low, moves, _ in low_rounds:
        digit = index >> low & len(moves)
        for move in moves:
            arrived = lax.ppermute(
                message, DEVICES, [(i, target(i, size, low, move)) for i in range(size)]
            ).astype(F32)
            before = place_among(digit, [move.index(place) for place in range(len(move))]) < digit
            earlier = earlier + jnp.where(before, arrived[0], 0.0)
            later = later + jnp.where(before, 0.0, arrived[1])
            total = total + arrived
        message = total.astype(BF16)
    low, moves, _ = top_round
    digit = index >> low & len(moves)
    messages = [jnp.where(place_among(digit, move) > digit, message[0], message[1]) for move in moves]
    messages = lax.optimization_barrier(tuple(messages))
    for move, message in zip(moves, messages):
        arrived = lax.ppermute(
            message, DEVICES, [(i, target(i, size, low, move)) for i in range(size)]
        ).astype(F32)
        before = place_among(digit, [move.index(place) for place in range(len(move))]) < digit
        earlier = earlier + jnp.where(before, arrived, 0.0)
        later = later + jnp.where(before, 0.0, arrived)
    first = index & 1 == 0
    mine = jnp.stack([earlier + jnp.where(first, 0.0, got[0]), later + jnp.where(first, got[1], 0.0)])
    theirs = jnp.stack([earlier + jnp.where(first, keep[0], 0.0), later + jnp.where(first, 0.0, keep[1])])
    return local, mine.astype(BF16), lax.ppermute(theirs.astype(BF16), DEVICES, swap)


def body(queries, keys, values, out_grad):
    kv = keys.shape[1] // HD
    shape = (2, kv // 2, HD, HD)
    vmem = pl.BlockSpec(memory_space=pltpu.VMEM)
    anywhere = pl.BlockSpec(memory_space=pltpu.HBM)
    inputs = (queries, keys, values, out_grad)
    tokens, wide, narrow = queries.shape[0], queries.shape[1], keys.shape[1]
    ordered = (keys, values, out_grad, queries)
    halves = [pltpu.VMEM((x.shape[0], x.shape[1] // 2), BF16) for x in ordered]
    send = pl.pallas_call(
        send_kernel,
        out_shape=jax.ShapeDtypeStruct(shape, BF16),
        in_specs=[anywhere] * 4,
        out_specs=vmem,
        scratch_shapes=halves + [pltpu.SemaphoreType.DMA((4,))],
        compiler_params=pltpu.CompilerParams(vmem_limit_bytes=55144 * 1024),
    )(*ordered)

    def keep():
        return pl.pallas_call(
            keep_kernel,
            out_shape=jax.ShapeDtypeStruct(shape, BF16),
            in_specs=[vmem] * 4,
            out_specs=vmem,
            cost_estimate=pl.CostEstimate(
                flops=2 * tokens * HD * wide, bytes_accessed=4 * tokens * wide, transcendentals=0
            ),
            compiler_params=pltpu.CompilerParams(vmem_limit_bytes=24 * MIB),
        )(*ordered)

    local_terms = pl.pallas_call(
        local_kernel,
        out_shape=tuple(jax.ShapeDtypeStruct(x.shape, F32) for x in (queries, keys, values))
        + (jax.ShapeDtypeStruct(out_grad.shape, BF16), jax.ShapeDtypeStruct(shape, F32)),
        in_specs=[vmem] * 6,
        out_specs=[vmem] * 5,
        cost_estimate=pl.CostEstimate(
            flops=12 * tokens * tokens * wide, bytes_accessed=12 * tokens * wide, transcendentals=0
        ),
        compiler_params=pltpu.CompilerParams(vmem_limit_bytes=24 * MIB),
    )
    (*local, scaled), mine, other = carry_states(keep, send, functools.partial(local_terms, *inputs))

    def finish(mine, state, *written):
        return pl.pallas_call(
            functools.partial(finish_kernel, mine),
            out_shape=tuple(jax.ShapeDtypeStruct(x.shape, BF16) for x in (queries, keys, values)),
            in_specs=[vmem] * 7 + [anywhere] * len(written),
            out_specs=[anywhere] * 3,
            scratch_shapes=[pltpu.VMEM(x.shape, BF16) for x in (queries, keys, values)]
            + [pltpu.SemaphoreType.DMA((3,))],
            input_output_aliases={7 + i: i for i in range(len(written))},
            cost_estimate=pl.CostEstimate(
                flops=4 * tokens * HD * wide, bytes_accessed=4 * tokens * wide, transcendentals=0
            ),
            compiler_params=pltpu.CompilerParams(vmem_limit_bytes=24 * MIB),
        )(keys, values, scaled, *local, state, *written)

    return finish(False, other, *finish(True, mine))


def solution(mesh):
    spec = P(DEVICES, None)
    return jax.shard_map(
        body, mesh=mesh, in_specs=(spec,) * 4, out_specs=(spec,) * 3, check_vma=False
    )
```

```python
import functools

import jax
import jax.numpy as jnp
from jax import lax
from jax.experimental import pallas as pl
from jax.experimental.pallas import tpu as pltpu
from jax.sharding import PartitionSpec as P

HD = 128
SEQ = "seq"
HEAD = "head"
DEVICES = (SEQ, HEAD)
LOW_MOVES = ((1, 0, 3, 2), (3, 2, 1, 0), (2, 3, 0, 1)), ((3, 2, 1, 0), (2, 3, 0, 1), (1, 0, 3, 2))
TOP_MOVES = ((1, 2, 3, 0), (2, 3, 0, 1), (3, 0, 1, 2)), ((1, 3, 0, 2), (3, 2, 0, 1), (2, 0, 3, 1))
LOW_ODD = (0, 1, 1, 0)
TOP_ODD = (0, 1, 0, 1)
MIB = 1024 * 1024
BF16 = jnp.bfloat16
F32 = jnp.float32

NN = (((1,), (0,)), ((), ()))
NT = (((1,), (1,)), ((), ()))
TN = (((0,), (0,)), ((), ()))


def dot(left, right, dims):
    return lax.dot_general(left, right, dims, preferred_element_type=F32)


def columns(index):
    return (slice(None), slice(index * HD, (index + 1) * HD))


def device_index():
    return lax.axis_index(SEQ) * lax.axis_size(HEAD) + lax.axis_index(HEAD)


def row_scale(tokens, shape, axis):
    positions = device_index() * tokens + lax.broadcasted_iota(jnp.int32, shape, axis)
    return 1.0 / jnp.sqrt((HD * (positions + 1)).astype(F32))


def prior_terms(k_ref, v_ref, out_ref):
    for g in range(out_ref.shape[0]):
        out_ref[g] = dot(v_ref[columns(g)], k_ref[columns(g)], TN).astype(BF16)


def future_terms(o_ref, q_ref, out_ref):
    tokens = q_ref.shape[0]
    kv = out_ref.shape[0]
    group = q_ref.shape[1] // HD // kv
    scale = row_scale(tokens, (tokens, HD), 0)
    for g in range(kv):
        grad = jnp.zeros((HD, HD), F32)
        for h in range(g * group, (g + 1) * group):
            scaled = (scale * o_ref[columns(h)].astype(F32)).astype(BF16)
            grad = grad + dot(scaled, q_ref[columns(h)], TN)
        out_ref[g] = grad.astype(BF16)


def my_side():
    return side_of(device_index(), lax.axis_size(SEQ) * lax.axis_size(HEAD))


def fetch(pairs, sems):
    copies = [pltpu.make_async_copy(source, place, sems.at[i]) for i, (source, place) in enumerate(pairs)]
    for copy in copies:
        copy.start(priority=1)
    for copy in copies:
        copy.wait()


def send_kernel(k_hbm, v_hbm, o_hbm, q_hbm, out_ref, k_ref, v_ref, o_ref, q_ref, sems):
    side = my_side()

    @pl.when(side == 1)
    def _():
        fetch([(o_hbm, o_ref), (q_hbm, q_ref)], sems)
        future_terms(o_ref, q_ref, out_ref)

    @pl.when(side == 0)
    def _():
        fetch([(k_hbm, k_ref), (v_hbm, v_ref)], sems)
        prior_terms(k_ref, v_ref, out_ref)


def keep_kernel(k_ref, v_ref, o_ref, q_ref, out_ref):
    side = my_side()

    @pl.when(side == 1)
    def _():
        prior_terms(k_ref, v_ref, out_ref)

    @pl.when(side == 0)
    def _():
        future_terms(o_ref, q_ref, out_ref)


def local_kernel(
    q_ref, k_ref, v_ref, o_ref, keep_ref, got_ref, qg_ref, kg_ref, vg_ref, scaled_ref, total_ref
):
    total_ref[...] = keep_ref[...].astype(F32) + got_ref[...].astype(F32)
    tokens = q_ref.shape[0]
    kv = k_ref.shape[1] // HD
    group = q_ref.shape[1] // HD // kv
    scale = row_scale(tokens, (tokens, HD), 0)
    scale_row = row_scale(tokens, (HD, tokens), 1)
    rows = lax.broadcasted_iota(jnp.int32, (tokens, tokens), 0)
    cols = lax.broadcasted_iota(jnp.int32, (tokens, tokens), 1)
    causal = rows >= cols
    causal_t = rows <= cols
    for g in range(kv):
        key = k_ref[columns(g)]
        value = v_ref[columns(g)]
        key_grad = jnp.zeros((tokens, HD), F32)
        value_grad = jnp.zeros((tokens, HD), F32)
        for h in range(g * group, (g + 1) * group):
            query = q_ref[columns(h)]
            cot = o_ref[columns(h)]
            scaled = (scale * cot.astype(F32)).astype(BF16)
            scaled_ref[columns(h)] = scaled
            backward = jnp.where(causal, dot(scaled, value, NT), 0.0).astype(BF16)
            backward_t = jnp.where(causal_t, dot(value, scaled, NT), 0.0).astype(BF16)
            forward_t = jnp.where(causal_t, scale_row * dot(key, query, NT), 0.0).astype(BF16)
            qg_ref[columns(h)] = dot(backward, key, NN)
            key_grad = key_grad + dot(backward_t, query, NN)
            value_grad = value_grad + dot(forward_t, cot, NN)
        kg_ref[columns(g)] = key_grad
        vg_ref[columns(g)] = value_grad


def finish_kernel(mine, k_ref, v_ref, scaled_ref, ql_ref, kl_ref, vl_ref, state_ref, *refs):
    qg_hbm, kg_hbm, vg_hbm, qg_ref, kg_ref, vg_ref, sems = refs[-7:]
    kv = k_ref.shape[1] // HD
    width = scaled_ref.shape[1] // kv
    side = my_side()

    def send(ref, hbm, at, sem):
        copy = pltpu.make_async_copy(ref.at[at], hbm.at[at], sems.at[sem])
        copy.start()
        return copy

    @pl.when(side == (1 if mine else 0))
    def _():
        copies = []
        for g in range(kv):
            for h in range(g * width // HD, (g + 1) * width // HD):
                qg_ref[columns(h)] = (
                    ql_ref[columns(h)] + dot(scaled_ref[columns(h)], state_ref[g], NN)
                ).astype(BF16)
            copies.append(send(qg_ref, qg_hbm, (slice(None), slice(g * width, (g + 1) * width)), g))
        for copy in copies:
            copy.wait()

    @pl.when(side == (0 if mine else 1))
    def _():
        for g in range(kv):
            key_grad = kl_ref[columns(g)] + dot(v_ref[columns(g)], state_ref[g], NN)
            value_grad = vl_ref[columns(g)] + dot(k_ref[columns(g)], state_ref[g], NT)
            kg_ref[columns(g)] = key_grad.astype(BF16)
            vg_ref[columns(g)] = value_grad.astype(BF16)
        copies = [send(kg_ref, kg_hbm, (slice(None),), 0), send(vg_ref, vg_hbm, (slice(None),), 1)]
        for copy in copies:
            copy.wait()


def digits(size):
    bits = size.bit_length() - 1
    assert 1 << bits == size
    return [(low, min(2, bits - low)) for low in range(1, bits, 2)]


def tables(size):
    found = []
    for low, width in digits(size):
        moves, odd = (LOW_MOVES, LOW_ODD) if low + width < size.bit_length() - 1 else (TOP_MOVES, TOP_ODD)
        found.append((low, moves, odd) if width == 2 else (low, (((1, 0),),) * 2, (0, 1)))
    return found


def side_of(index, size):
    side = index & 1
    for low, _, odd in tables(size):
        digit = index >> low & len(odd) - 1
        for place in range(len(odd)):
            if odd[place]:
                side = side ^ (digit == place)
    return side


def target(index, size, low, move):
    digit = index >> low & len(move) - 1
    other = index ^ (digit ^ move[digit]) << low
    return other ^ side_of(other, size) ^ side_of(index, size)


def place_among(digit, places):
    found = places[0]
    for place, other in enumerate(places):
        found = jnp.where(digit == place, other, found)
    return found


def new_pairs(moves, n):
    return [all(move[place] != moves[n][place] for move in moves[:n]) for place in range(len(moves[n]))]


def carry_states(send, keep_states, local_terms):
    size = lax.axis_size(SEQ) * lax.axis_size(HEAD)
    index = device_index()
    side = side_of(index, size)
    future = side == 0
    swap = [(i, i ^ 1) for i in range(size)]
    got = lax.ppermute(send, DEVICES, swap)
    keep = keep_states()
    *local, chip = local_terms(keep, got)
    keep = keep.astype(F32)
    got = got.astype(F32)
    own = keep + got
    total = own
    carried = 0.0
    rounds = tables(size)
    for step, ways in enumerate(zip(rounds, rounds[::-1])):
        (future_low, (future_moves, _), _), (prior_low, (_, prior_moves), _) = ways
        future_digit = index >> future_low & len(future_moves[0]) - 1
        prior_digit = index >> prior_low & len(prior_moves[0]) - 1
        messages = []
        for n in range(max(len(future_moves), len(prior_moves))):
            message = total
            if n < len(prior_moves):
                wanted = new_pairs(prior_moves, n)
                earlier = (prior_digit < place_among(prior_digit, prior_moves[n])) & place_among(prior_digit, wanted)
                message = jnp.where(future, total, carried + jnp.where(earlier, own, 0.0))
                if step > 0:
                    message = jnp.where(future | place_among(prior_digit, wanted), message, 0.0)
            messages.append(message.astype(BF16))
        messages = lax.optimization_barrier(tuple(messages))
        if step == 0:
            total = chip
            own = chip
        for n, message in enumerate(messages):
            perm = []
            for i in range(size):
                at = side_of(i, size)
                low, moves = ways[at][0], ways[at][1][at]
                if n < len(moves):
                    perm.append((i, target(i, size, low, moves[n])))
            arrived = lax.ppermute(message, DEVICES, perm).astype(F32)
            wanted = side == 1
            if n < len(future_moves):
                source = [future_moves[n].index(place) for place in range(len(future_moves[n]))]
                new = [new_pairs(future_moves, n)[place] for place in source]
                fresh = place_among(future_digit, new)
                wanted = wanted | (place_among(future_digit, source) > future_digit) & fresh
                total = total + jnp.where(fresh, arrived, 0.0)
            carried = carried + jnp.where(wanted, arrived, 0.0)
    first = index & 1 == 0
    mine = carried + jnp.where(first == future, got, 0.0)
    theirs = carried + jnp.where(first == (side == 1), keep, 0.0)
    return local, mine.astype(BF16), lax.ppermute(theirs.astype(BF16), DEVICES, swap)


def body(queries, keys, values, out_grad):
    kv = keys.shape[1] // HD
    shape = (kv, HD, HD)
    vmem = pl.BlockSpec(memory_space=pltpu.VMEM)
    anywhere = pl.BlockSpec(memory_space=pltpu.HBM)
    inputs = (queries, keys, values, out_grad)
    tokens, wide, narrow = queries.shape[0], queries.shape[1], keys.shape[1]
    ordered = (keys, values, out_grad, queries)
    send = pl.pallas_call(
        send_kernel,
        out_shape=jax.ShapeDtypeStruct(shape, BF16),
        in_specs=[anywhere] * 4,
        out_specs=vmem,
        scratch_shapes=[pltpu.VMEM(x.shape, BF16) for x in ordered] + [pltpu.SemaphoreType.DMA((2,))],
        compiler_params=pltpu.CompilerParams(vmem_limit_bytes=55144 * 1024),
    )(*ordered)

    def keep_states():
        return pl.pallas_call(
            keep_kernel,
            out_shape=jax.ShapeDtypeStruct(shape, BF16),
            in_specs=[vmem] * 4,
            out_specs=vmem,
            cost_estimate=pl.CostEstimate(
                flops=2 * tokens * HD * wide, bytes_accessed=4 * tokens * wide, transcendentals=0
            ),
            compiler_params=pltpu.CompilerParams(vmem_limit_bytes=24 * MIB),
        )(*ordered)

    local_terms = pl.pallas_call(
        local_kernel,
        out_shape=tuple(jax.ShapeDtypeStruct(x.shape, F32) for x in (queries, keys, values))
        + (jax.ShapeDtypeStruct(out_grad.shape, BF16), jax.ShapeDtypeStruct(shape, F32)),
        in_specs=[vmem] * 6,
        out_specs=[vmem] * 5,
        cost_estimate=pl.CostEstimate(
            flops=12 * tokens * tokens * wide, bytes_accessed=12 * tokens * wide, transcendentals=0
        ),
        compiler_params=pltpu.CompilerParams(vmem_limit_bytes=24 * MIB),
    )
    (*local, scaled), mine, other = carry_states(send, keep_states, functools.partial(local_terms, *inputs))

    def finish(mine, state, *written):
        return pl.pallas_call(
            functools.partial(finish_kernel, mine),
            out_shape=tuple(jax.ShapeDtypeStruct(x.shape, BF16) for x in (queries, keys, values)),
            in_specs=[vmem] * 7 + [anywhere] * len(written),
            out_specs=[anywhere] * 3,
            scratch_shapes=[pltpu.VMEM(x.shape, BF16) for x in (queries, keys, values)]
            + [pltpu.SemaphoreType.DMA((kv,))],
            input_output_aliases={7 + i: i for i in range(len(written))},
            cost_estimate=pl.CostEstimate(
                flops=4 * tokens * HD * wide, bytes_accessed=4 * tokens * wide, transcendentals=0
            ),
            compiler_params=pltpu.CompilerParams(vmem_limit_bytes=24 * MIB),
        )(keys, values, scaled, *local, state, *written)

    return finish(False, other, *finish(True, mine))


def solution(mesh):
    spec = P(DEVICES, None)
    return jax.shard_map(
        body, mesh=mesh, in_specs=(spec,) * 4, out_specs=(spec,) * 3, check_vma=False
    )
```

```python
import functools

import jax
import jax.numpy as jnp
from jax import lax
from jax.experimental import pallas as pl
from jax.experimental.pallas import tpu as pltpu
from jax.sharding import PartitionSpec as P

HD = 128
SEQ = "seq"
HEAD = "head"
DEVICES = (SEQ, HEAD)
LOW_MOVES = ((1, 0, 3, 2), (3, 2, 1, 0), (2, 3, 0, 1))
TOP_MOVES = ((3, 0, 1, 2), (2, 3, 0, 1), (1, 2, 3, 0))
LOW_ODD = (0, 1, 1, 0)
TOP_ODD = (0, 1, 0, 1)
MIB = 1024 * 1024
BF16 = jnp.bfloat16
F32 = jnp.float32

NN = (((1,), (0,)), ((), ()))
NT = (((1,), (1,)), ((), ()))
TN = (((0,), (0,)), ((), ()))


def dot(left, right, dims):
    return lax.dot_general(left, right, dims, preferred_element_type=F32)


def columns(index):
    return (slice(None), slice(index * HD, (index + 1) * HD))


def device_index():
    return lax.axis_index(SEQ) * lax.axis_size(HEAD) + lax.axis_index(HEAD)


def row_scale(tokens, shape, axis):
    positions = device_index() * tokens + lax.broadcasted_iota(jnp.int32, shape, axis)
    return 1.0 / jnp.sqrt((HD * (positions + 1)).astype(F32))


def half_states(k_ref, v_ref, o_ref, q_ref, out_ref, copies=()):
    tokens = q_ref.shape[0]
    half = k_ref.shape[1] // HD
    group = q_ref.shape[1] // k_ref.shape[1]
    scale = row_scale(tokens, (tokens, HD), 0)
    for copy in copies[:2]:
        copy.wait()
    for g in range(half):
        out_ref[0, g] = dot(v_ref[columns(g)], k_ref[columns(g)], TN).astype(BF16)
    for copy in copies[2:]:
        copy.wait()
    for g in range(half):
        grad = jnp.zeros((HD, HD), F32)
        for h in range(g * group, (g + 1) * group):
            scaled = (scale * o_ref[columns(h)].astype(F32)).astype(BF16)
            grad = grad + dot(scaled, q_ref[columns(h)], TN)
        out_ref[1, g] = grad.astype(BF16)


def half_columns(ref, side):
    width = ref.shape[1] // 2
    return ref.at[:, pl.ds(pl.multiple_of(side * width, HD), width)]


def send_kernel(k_hbm, v_hbm, o_hbm, q_hbm, out_ref, k_ref, v_ref, o_ref, q_ref, sems):
    side = 1 - side_of(device_index(), lax.axis_size(SEQ) * lax.axis_size(HEAD))
    copies = [
        pltpu.make_async_copy(half_columns(source, side), place, sems.at[i])
        for i, (source, place) in enumerate([(k_hbm, k_ref), (v_hbm, v_ref), (o_hbm, o_ref), (q_hbm, q_ref)])
    ]
    for copy in copies:
        copy.start(priority=1)
    half_states(k_ref, v_ref, o_ref, q_ref, out_ref, copies)


def keep_kernel(k_ref, v_ref, o_ref, q_ref, out_ref):
    side = side_of(device_index(), lax.axis_size(SEQ) * lax.axis_size(HEAD))
    half_states(*[half_columns(ref, side) for ref in (k_ref, v_ref, o_ref, q_ref)], out_ref)


def local_kernel(
    q_ref, k_ref, v_ref, o_ref, keep_ref, got_ref, qg_ref, kg_ref, vg_ref, scaled_ref, total_ref
):
    total_ref[...] = keep_ref[...].astype(F32) + got_ref[...].astype(F32)
    tokens = q_ref.shape[0]
    kv = k_ref.shape[1] // HD
    group = q_ref.shape[1] // HD // kv
    scale = row_scale(tokens, (tokens, HD), 0)
    scale_row = row_scale(tokens, (HD, tokens), 1)
    rows = lax.broadcasted_iota(jnp.int32, (tokens, tokens), 0)
    cols = lax.broadcasted_iota(jnp.int32, (tokens, tokens), 1)
    causal = rows >= cols
    causal_t = rows <= cols
    for g in range(kv):
        key = k_ref[columns(g)]
        value = v_ref[columns(g)]
        key_grad = jnp.zeros((tokens, HD), F32)
        value_grad = jnp.zeros((tokens, HD), F32)
        for h in range(g * group, (g + 1) * group):
            query = q_ref[columns(h)]
            cot = o_ref[columns(h)]
            scaled = (scale * cot.astype(F32)).astype(BF16)
            scaled_ref[columns(h)] = scaled
            backward = jnp.where(causal, dot(scaled, value, NT), 0.0).astype(BF16)
            backward_t = jnp.where(causal_t, dot(value, scaled, NT), 0.0).astype(BF16)
            forward_t = jnp.where(causal_t, scale_row * dot(key, query, NT), 0.0).astype(BF16)
            qg_ref[columns(h)] = dot(backward, key, NN)
            key_grad = key_grad + dot(backward_t, query, NN)
            value_grad = value_grad + dot(forward_t, cot, NN)
        kg_ref[columns(g)] = key_grad
        vg_ref[columns(g)] = value_grad


def finish_kernel(mine, k_ref, v_ref, scaled_ref, ql_ref, kl_ref, vl_ref, state_ref, *refs):
    qg_hbm, kg_hbm, vg_hbm, qg_ref, kg_ref, vg_ref, sems = refs[-7:]
    tokens = scaled_ref.shape[0]
    kv = k_ref.shape[1] // HD
    width = scaled_ref.shape[1] // kv
    group = width // HD
    half = kv // 2
    side = side_of(device_index(), lax.axis_size(SEQ) * lax.axis_size(HEAD))

    def finish(part):
        copies = []

        def send(ref, hbm, low, size):
            at = (slice(None), slice(low, low + size))
            copies.append(pltpu.make_async_copy(ref.at[at], hbm.at[at], sems.at[len(copies)]))
            copies[-1].start()

        for g in range(part * half, (part + 1) * half):
            prior = state_ref[0, g % half]
            for h in range(g * group, (g + 1) * group):
                scaled = scaled_ref[columns(h)]
                qg_ref[columns(h)] = (ql_ref[columns(h)] + dot(scaled, prior, NN)).astype(BF16)
        send(qg_ref, qg_hbm, part * half * width, half * width)
        for g in range(part * half, (part + 1) * half):
            future = state_ref[1, g % half]
            key_grad = kl_ref[columns(g)] + dot(v_ref[columns(g)], future, NN)
            value_grad = vl_ref[columns(g)] + dot(k_ref[columns(g)], future, NT)
            kg_ref[columns(g)] = key_grad.astype(BF16)
            vg_ref[columns(g)] = value_grad.astype(BF16)
        send(kg_ref, kg_hbm, part * half * HD, half * HD)
        send(vg_ref, vg_hbm, part * half * HD, half * HD)
        for copy in copies:
            copy.wait()

    for part in range(2):
        pl.when(side == (part if mine else 1 - part))(functools.partial(finish, part))


def digits(size):
    bits = size.bit_length() - 1
    assert 1 << bits == size
    return [(low, min(2, bits - low)) for low in range(1, bits, 2)]


def tables(size):
    found = []
    for low, width in digits(size):
        moves, odd = (LOW_MOVES, LOW_ODD) if low + width < size.bit_length() - 1 else (TOP_MOVES, TOP_ODD)
        found.append((low, moves, odd) if width == 2 else (low, ((1, 0),), (0, 1)))
    return found


def side_of(index, size):
    side = index & 1
    for low, moves, odd in tables(size):
        digit = index >> low & len(odd) - 1
        for place in range(len(odd)):
            if odd[place]:
                side = side ^ (digit == place)
    return side


def target(index, size, low, move):
    digit = index >> low & len(move) - 1
    other = index ^ (digit ^ move[digit]) << low
    return other ^ side_of(other, size) ^ side_of(index, size)


def place_among(digit, places):
    return sum(jnp.where(digit == place, other, 0) for place, other in enumerate(places))


def carry_states(keep, send, local_terms):
    size = lax.axis_size(SEQ) * lax.axis_size(HEAD)
    index = device_index()
    swap = [(i, i ^ 1) for i in range(size)]
    got = lax.ppermute(send, DEVICES, swap)
    keep = keep()
    *local, total = local_terms(keep, got)
    keep = keep.astype(F32)
    got = got.astype(F32)
    message = (keep + got).astype(BF16)
    low_rounds, (top, moves, _) = tables(size)[:-1], tables(size)[-1]

    def exchange(messages, low, moves):
        digit = index >> low & len(moves)
        found = []
        for move, message in zip(moves, lax.optimization_barrier(tuple(messages))):
            perm = [(i, target(i, size, low, move)) for i in range(size)]
            source = place_among(digit, [move.index(place) for place in range(len(move))])
            found.append((source < digit, lax.ppermute(message, DEVICES, perm).astype(F32)))
        return found

    def upward(low, move):
        digit = index >> low & len(move) - 1
        return place_among(digit, move) > digit

    messages = [jnp.where(upward(top, move), message[0], message[1]) for move in moves]
    earlier, later = 0.0, 0.0
    for before, arrived in exchange(messages, top, moves):
        earlier = earlier + jnp.where(before, arrived, 0.0)
        later = later + jnp.where(before, 0.0, arrived)
    for low, moves, _ in low_rounds[::-1]:
        up = jnp.stack([earlier + total[0], later]).astype(BF16)
        down = jnp.stack([earlier, later + total[1]]).astype(BF16)
        messages = [jnp.where(upward(low, move), up, down) for move in moves]
        for _, arrived in exchange(messages, low, moves):
            earlier = earlier + arrived[0]
            later = later + arrived[1]
    first = index & 1 == 0
    mine = jnp.stack([earlier + jnp.where(first, 0.0, got[0]), later + jnp.where(first, got[1], 0.0)])
    theirs = jnp.stack([earlier + jnp.where(first, keep[0], 0.0), later + jnp.where(first, 0.0, keep[1])])
    return local, mine.astype(BF16), lax.ppermute(theirs.astype(BF16), DEVICES, swap)


def body(queries, keys, values, out_grad):
    kv = keys.shape[1] // HD
    shape = (2, kv // 2, HD, HD)
    vmem = pl.BlockSpec(memory_space=pltpu.VMEM)
    anywhere = pl.BlockSpec(memory_space=pltpu.HBM)
    inputs = (queries, keys, values, out_grad)
    tokens, wide, narrow = queries.shape[0], queries.shape[1], keys.shape[1]
    ordered = (keys, values, out_grad, queries)
    halves = [pltpu.VMEM((x.shape[0], x.shape[1] // 2), BF16) for x in ordered]
    send = pl.pallas_call(
        send_kernel,
        out_shape=jax.ShapeDtypeStruct(shape, BF16),
        in_specs=[anywhere] * 4,
        out_specs=vmem,
        scratch_shapes=halves + [pltpu.SemaphoreType.DMA((4,))],
        compiler_params=pltpu.CompilerParams(vmem_limit_bytes=55144 * 1024),
    )(*ordered)

    def keep():
        return pl.pallas_call(
            keep_kernel,
            out_shape=jax.ShapeDtypeStruct(shape, BF16),
            in_specs=[vmem] * 4,
            out_specs=vmem,
            cost_estimate=pl.CostEstimate(
                flops=2 * tokens * HD * wide, bytes_accessed=4 * tokens * wide, transcendentals=0
            ),
            compiler_params=pltpu.CompilerParams(vmem_limit_bytes=24 * MIB),
        )(*ordered)

    local_terms = pl.pallas_call(
        local_kernel,
        out_shape=tuple(jax.ShapeDtypeStruct(x.shape, F32) for x in (queries, keys, values))
        + (jax.ShapeDtypeStruct(out_grad.shape, BF16), jax.ShapeDtypeStruct(shape, F32)),
        in_specs=[vmem] * 6,
        out_specs=[vmem] * 5,
        cost_estimate=pl.CostEstimate(
            flops=12 * tokens * tokens * wide, bytes_accessed=12 * tokens * wide, transcendentals=0
        ),
        compiler_params=pltpu.CompilerParams(vmem_limit_bytes=24 * MIB),
    )
    (*local, scaled), mine, other = carry_states(keep, send, functools.partial(local_terms, *inputs))

    def finish(mine, state, *written):
        return pl.pallas_call(
            functools.partial(finish_kernel, mine),
            out_shape=tuple(jax.ShapeDtypeStruct(x.shape, BF16) for x in (queries, keys, values)),
            in_specs=[vmem] * 7 + [anywhere] * len(written),
            out_specs=[anywhere] * 3,
            scratch_shapes=[pltpu.VMEM(x.shape, BF16) for x in (queries, keys, values)]
            + [pltpu.SemaphoreType.DMA((3,))],
            input_output_aliases={7 + i: i for i in range(len(written))},
            cost_estimate=pl.CostEstimate(
                flops=4 * tokens * HD * wide, bytes_accessed=4 * tokens * wide, transcendentals=0
            ),
            compiler_params=pltpu.CompilerParams(vmem_limit_bytes=24 * MIB),
        )(keys, values, scaled, *local, state, *written)

    return finish(False, other, *finish(True, mine))


def solution(mesh):
    spec = P(DEVICES, None)
    return jax.shard_map(
        body, mesh=mesh, in_specs=(spec,) * 4, out_specs=(spec,) * 3, check_vma=False
    )
```

```python
import functools

import jax
import jax.numpy as jnp
from jax import lax
from jax.experimental import pallas as pl
from jax.experimental.pallas import tpu as pltpu
from jax.sharding import PartitionSpec as P

HD = 128
SEQ = "seq"
HEAD = "head"
DEVICES = (SEQ, HEAD)
LOW_MOVES = ((1, 0, 3, 2), (3, 2, 1, 0), (2, 3, 0, 1))
TOP_MOVES = ((3, 0, 1, 2), (2, 3, 0, 1), (1, 2, 3, 0))
LOW_ODD = (0, 1, 1, 0)
TOP_ODD = (0, 1, 0, 1)
MIB = 1024 * 1024
BF16 = jnp.bfloat16
F32 = jnp.float32

NN = (((1,), (0,)), ((), ()))
NT = (((1,), (1,)), ((), ()))
TN = (((0,), (0,)), ((), ()))


def dot(left, right, dims):
    return lax.dot_general(left, right, dims, preferred_element_type=F32)


def columns(index):
    return (slice(None), slice(index * HD, (index + 1) * HD))


def device_index():
    return lax.axis_index(SEQ) * lax.axis_size(HEAD) + lax.axis_index(HEAD)


def row_scale(tokens, shape, axis):
    positions = device_index() * tokens + lax.broadcasted_iota(jnp.int32, shape, axis)
    return 1.0 / jnp.sqrt((HD * (positions + 1)).astype(F32))


def half_states(k_ref, v_ref, o_ref, q_ref, out_ref, copies=()):
    tokens = q_ref.shape[0]
    half = k_ref.shape[1] // HD
    group = q_ref.shape[1] // k_ref.shape[1]
    scale = row_scale(tokens, (tokens, HD), 0)
    for copy in copies[:2]:
        copy.wait()
    for g in range(half):
        out_ref[0, g] = dot(v_ref[columns(g)], k_ref[columns(g)], TN).astype(BF16)
    for copy in copies[2:]:
        copy.wait()
    for g in range(half):
        grad = jnp.zeros((HD, HD), F32)
        for h in range(g * group, (g + 1) * group):
            scaled = (scale * o_ref[columns(h)].astype(F32)).astype(BF16)
            grad = grad + dot(scaled, q_ref[columns(h)], TN)
        out_ref[1, g] = grad.astype(BF16)


def half_columns(ref, side):
    width = ref.shape[1] // 2
    return ref.at[:, pl.ds(pl.multiple_of(side * width, HD), width)]


def send_kernel(k_hbm, v_hbm, o_hbm, q_hbm, out_ref, k_ref, v_ref, o_ref, q_ref, sems):
    side = 1 - side_of(device_index(), lax.axis_size(SEQ) * lax.axis_size(HEAD))
    copies = [
        pltpu.make_async_copy(half_columns(source, side), place, sems.at[i])
        for i, (source, place) in enumerate([(k_hbm, k_ref), (v_hbm, v_ref), (o_hbm, o_ref), (q_hbm, q_ref)])
    ]
    for copy in copies:
        copy.start(priority=1)
    half_states(k_ref, v_ref, o_ref, q_ref, out_ref, copies)


def keep_kernel(k_ref, v_ref, o_ref, q_ref, out_ref):
    side = side_of(device_index(), lax.axis_size(SEQ) * lax.axis_size(HEAD))
    half_states(*[half_columns(ref, side) for ref in (k_ref, v_ref, o_ref, q_ref)], out_ref)


def local_kernel(
    q_ref, k_ref, v_ref, o_ref, keep_ref, got_ref, qg_ref, kg_ref, vg_ref, scaled_ref, total_ref
):
    total_ref[...] = keep_ref[...].astype(F32) + got_ref[...].astype(F32)
    tokens = q_ref.shape[0]
    kv = k_ref.shape[1] // HD
    group = q_ref.shape[1] // HD // kv
    scale = row_scale(tokens, (tokens, HD), 0)
    scale_row = row_scale(tokens, (HD, tokens), 1)
    rows = lax.broadcasted_iota(jnp.int32, (tokens, tokens), 0)
    cols = lax.broadcasted_iota(jnp.int32, (tokens, tokens), 1)
    causal = rows >= cols
    causal_t = rows <= cols
    for g in range(kv):
        key = k_ref[columns(g)]
        value = v_ref[columns(g)]
        key_grad = jnp.zeros((tokens, HD), F32)
        value_grad = jnp.zeros((tokens, HD), F32)
        for h in range(g * group, (g + 1) * group):
            query = q_ref[columns(h)]
            cot = o_ref[columns(h)]
            scaled = (scale * cot.astype(F32)).astype(BF16)
            scaled_ref[columns(h)] = scaled
            backward = jnp.where(causal, dot(scaled, value, NT), 0.0).astype(BF16)
            backward_t = jnp.where(causal_t, dot(value, scaled, NT), 0.0).astype(BF16)
            forward_t = jnp.where(causal_t, scale_row * dot(key, query, NT), 0.0).astype(BF16)
            qg_ref[columns(h)] = dot(backward, key, NN)
            key_grad = key_grad + dot(backward_t, query, NN)
            value_grad = value_grad + dot(forward_t, cot, NN)
        kg_ref[columns(g)] = key_grad
        vg_ref[columns(g)] = value_grad


def finish_kernel(mine, k_ref, v_ref, scaled_ref, ql_ref, kl_ref, vl_ref, state_ref, *refs):
    qg_hbm, kg_hbm, vg_hbm, qg_ref, kg_ref, vg_ref, sems = refs[-7:]
    tokens = scaled_ref.shape[0]
    kv = k_ref.shape[1] // HD
    width = scaled_ref.shape[1] // kv
    group = width // HD
    half = kv // 2
    side = side_of(device_index(), lax.axis_size(SEQ) * lax.axis_size(HEAD))

    def finish(part):
        copies = []

        def send(ref, hbm, low, size):
            at = (slice(None), slice(low, low + size))
            copies.append(pltpu.make_async_copy(ref.at[at], hbm.at[at], sems.at[len(copies)]))
            copies[-1].start()

        for g in range(part * half, (part + 1) * half):
            prior = state_ref[0, g % half]
            for h in range(g * group, (g + 1) * group):
                scaled = scaled_ref[columns(h)]
                qg_ref[columns(h)] = (ql_ref[columns(h)] + dot(scaled, prior, NN)).astype(BF16)
        send(qg_ref, qg_hbm, part * half * width, half * width)
        for g in range(part * half, (part + 1) * half):
            future = state_ref[1, g % half]
            key_grad = kl_ref[columns(g)] + dot(v_ref[columns(g)], future, NN)
            value_grad = vl_ref[columns(g)] + dot(k_ref[columns(g)], future, NT)
            kg_ref[columns(g)] = key_grad.astype(BF16)
            vg_ref[columns(g)] = value_grad.astype(BF16)
        send(kg_ref, kg_hbm, part * half * HD, half * HD)
        send(vg_ref, vg_hbm, part * half * HD, half * HD)
        for copy in copies:
            copy.wait()

    for part in range(2):
        pl.when(side == (part if mine else 1 - part))(functools.partial(finish, part))


def digits(size):
    bits = size.bit_length() - 1
    assert 1 << bits == size
    return [(low, min(2, bits - low)) for low in range(1, bits, 2)]


def tables(size):
    found = []
    for low, width in digits(size):
        moves, odd = (LOW_MOVES, LOW_ODD) if low + width < size.bit_length() - 1 else (TOP_MOVES, TOP_ODD)
        found.append((low, moves, odd) if width == 2 else (low, ((1, 0),), (0, 1)))
    return found


def side_of(index, size):
    side = index & 1
    for low, moves, odd in tables(size):
        digit = index >> low & len(odd) - 1
        for place in range(len(odd)):
            if odd[place]:
                side = side ^ (digit == place)
    return side


def target(index, size, low, move):
    digit = index >> low & len(move) - 1
    other = index ^ (digit ^ move[digit]) << low
    return other ^ side_of(other, size) ^ side_of(index, size)


def place_among(digit, places):
    return sum(jnp.where(digit == place, other, 0) for place, other in enumerate(places))


def carry_states(keep, send, local_terms):
    size = lax.axis_size(SEQ) * lax.axis_size(HEAD)
    index = device_index()
    swap = [(i, i ^ 1) for i in range(size)]
    got = lax.ppermute(send, DEVICES, swap)
    keep = keep()
    *local, total = local_terms(keep, got)
    keep = keep.astype(F32)
    got = got.astype(F32)
    message = (keep + got).astype(BF16)
    earlier = jnp.zeros_like(total[0])
    later = jnp.zeros_like(total[1])
    *low_rounds, top_round = tables(size)
    for low, moves, _ in low_rounds:
        digit = index >> low & len(moves)
        for move in moves:
            arrived = lax.ppermute(
                message, DEVICES, [(i, target(i, size, low, move)) for i in range(size)]
            ).astype(F32)
            before = place_among(digit, [move.index(place) for place in range(len(move))]) < digit
            earlier = earlier + jnp.where(before, arrived[0], 0.0)
            later = later + jnp.where(before, 0.0, arrived[1])
            total = total + arrived
        message = total.astype(BF16)
    low, moves, _ = top_round
    digit = index >> low & len(moves)
    messages = [jnp.where(place_among(digit, move) > digit, message[0], message[1]) for move in moves]
    messages = lax.optimization_barrier(tuple(messages))
    for move, message in zip(moves, messages):
        arrived = lax.ppermute(
            message, DEVICES, [(i, target(i, size, low, move)) for i in range(size)]
        ).astype(F32)
        before = place_among(digit, [move.index(place) for place in range(len(move))]) < digit
        earlier = earlier + jnp.where(before, arrived, 0.0)
        later = later + jnp.where(before, 0.0, arrived)
    first = index & 1 == 0
    mine = jnp.stack([earlier + jnp.where(first, 0.0, got[0]), later + jnp.where(first, got[1], 0.0)])
    theirs = jnp.stack([earlier + jnp.where(first, keep[0], 0.0), later + jnp.where(first, 0.0, keep[1])])
    return local, mine.astype(BF16), lax.ppermute(theirs.astype(BF16), DEVICES, swap)


def body(queries, keys, values, out_grad):
    kv = keys.shape[1] // HD
    shape = (2, kv // 2, HD, HD)
    vmem = pl.BlockSpec(memory_space=pltpu.VMEM)
    anywhere = pl.BlockSpec(memory_space=pltpu.HBM)
    inputs = (queries, keys, values, out_grad)
    tokens, wide, narrow = queries.shape[0], queries.shape[1], keys.shape[1]
    ordered = (keys, values, out_grad, queries)
    halves = [pltpu.VMEM((x.shape[0], x.shape[1] // 2), BF16) for x in ordered]
    send = pl.pallas_call(
        send_kernel,
        out_shape=jax.ShapeDtypeStruct(shape, BF16),
        in_specs=[anywhere] * 4,
        out_specs=vmem,
        scratch_shapes=halves + [pltpu.SemaphoreType.DMA((4,))],
        compiler_params=pltpu.CompilerParams(vmem_limit_bytes=55144 * 1024),
    )(*ordered)

    def keep():
        return pl.pallas_call(
            keep_kernel,
            out_shape=jax.ShapeDtypeStruct(shape, BF16),
            in_specs=[vmem] * 4,
            out_specs=vmem,
            cost_estimate=pl.CostEstimate(
                flops=2 * tokens * HD * wide, bytes_accessed=4 * tokens * wide, transcendentals=0
            ),
            compiler_params=pltpu.CompilerParams(vmem_limit_bytes=24 * MIB),
        )(*ordered)

    local_terms = pl.pallas_call(
        local_kernel,
        out_shape=tuple(jax.ShapeDtypeStruct(x.shape, F32) for x in (queries, keys, values))
        + (jax.ShapeDtypeStruct(out_grad.shape, BF16), jax.ShapeDtypeStruct(shape, F32)),
        in_specs=[vmem] * 6,
        out_specs=[vmem] * 5,
        cost_estimate=pl.CostEstimate(
            flops=12 * tokens * tokens * wide, bytes_accessed=12 * tokens * wide, transcendentals=0
        ),
        compiler_params=pltpu.CompilerParams(vmem_limit_bytes=24 * MIB),
    )
    (*local, scaled), mine, other = carry_states(keep, send, functools.partial(local_terms, *inputs))

    def finish(mine, state, *written):
        return pl.pallas_call(
            functools.partial(finish_kernel, mine),
            out_shape=tuple(jax.ShapeDtypeStruct(x.shape, BF16) for x in (queries, keys, values)),
            in_specs=[vmem] * 7 + [anywhere] * len(written),
            out_specs=[anywhere] * 3,
            scratch_shapes=[pltpu.VMEM(x.shape, BF16) for x in (queries, keys, values)]
            + [pltpu.SemaphoreType.DMA((3,))],
            input_output_aliases={7 + i: i for i in range(len(written))},
            cost_estimate=pl.CostEstimate(
                flops=4 * tokens * HD * wide, bytes_accessed=4 * tokens * wide, transcendentals=0
            ),
            compiler_params=pltpu.CompilerParams(vmem_limit_bytes=24 * MIB),
        )(keys, values, scaled, *local, state, *written)

    return finish(False, other, *finish(True, mine))


def solution(mesh):
    spec = P(DEVICES, None)
    return jax.shard_map(
        body, mesh=mesh, in_specs=(spec,) * 4, out_specs=(spec,) * 3, check_vma=False
    )
```
